32 devices in a mesh: groups: 2 (over y), row: 4 (over z), col: 4 (over x, core).
Axes of the slice: x: 2, y: 2, z: 4, core: 2. Of those that a mesh axis runs over, the one named last changes fastest.
Arguments:
- src_points: bfloat16 [256, 128, 64], P(('groups', 'row')), parts along dimension 0, may hold values from -8 to 8, as said below
- tgt_points: bfloat16 [1024, 128, 64], P(('groups', 'col')), parts along dimension 0, may hold values from -8 to 8, as said below
- src_logw: float32 [256, 128], P(('groups', 'row')), parts along dimension 0, may hold values from -1 to 1
- tgt_logw: float32 [1024, 128], P(('groups', 'col')), parts along dimension 0, may hold values from -1 to 1
- src_sizes: int32 [256], P(('groups', 'row')), parts along dimension 0, may hold values from 64 to 128, as said below
- tgt_sizes: int32 [1024], P(('groups', 'col')), parts along dimension 0, may hold values from 64 to 128, as said below
- pattern: int32 [256, 4, 8], P(('groups', 'row'), 'col'), parts along dimension 0, may hold values from 0 to 127, as said below
- counts: int32 [256, 4], P(('groups', 'row'), 'col'), parts along dimension 0, may hold values from 1 to 8, as said below
Outputs:
- field_f: float32 [256, 128], P(('groups', 'row')), parts along dimension 0
- field_g: float32 [1024, 128], P(('groups', 'col')), parts along dimension 0
The draws below stay inside these ranges and needn't reach their ends.
There are 2 independent parts, one for each index of `groups`. The reference program is written for one: setup_inputs(seed, part) draws one part's arguments, and reference() takes and returns one part's arrays. A program takes and returns all parts, laid end to end along the dimension named above; each array names one. Nothing has to cross between parts.
Inputs may be any that keep to these rules, and one draw needn't show every extreme that they name: `src_sizes`: real cells fill a block from slot 0; some block has exactly 128 and some exactly 64. `tgt_sizes`: real cells fill a block from slot 0; some block has exactly 128 and some exactly 64. The 8 entries of pattern[s, c] are distinct; in every column shard exactly two target blocks, never the first or the last of the shard, appear in no entry of pattern, so they have no neighbours. `counts`: every source block has at least one neighbour in every column shard; some pair (s, c) has 8. `src_points`: coordinates are cluster centres plus noise. `tgt_points`: coordinates are cluster centres plus noise.
All inputs are finite; a program needn't handle non-finite values.
Results may differ from the reference program's by a relative error of at most 0.0003.
Values sent between devices are 32-bit elements; how exact they have to be, the bound alone decides.
No kernel may reach another device: no remote copies, remote signals or barrier semaphores. Data moves between devices by JAX's collectives and lax.ppermute only.
A program may use at most 64 MiB of HBM per device.

```python
import math
import jax
import jax.numpy as jnp
from jax import lax

D = 64
BLK = 128
KMAX = 8
ITERS = 2
TB_DEV = 128
SBLOCKS = 128
TBLOCKS = 512
NCOLS = 4


def cloud(key, blocks, far_scale, far_share, noise_lo, noise_hi):
    key_c, key_f, key_m, key_n, key_s = jax.random.split(key, 5)
    centres = jax.random.normal(key_c, (blocks, 1, D), jnp.float32) * 0.15
    far_mask = jax.random.uniform(key_m, (blocks, 1, 1), jnp.float32) < far_share
    far_part = jnp.where(far_mask, far_scale, 0.0) * jax.random.normal(key_f, (blocks, 1, D), jnp.float32)
    spread = jnp.exp(jax.random.uniform(key_s, (blocks, 1, 1), jnp.float32, minval=math.log(noise_lo), maxval=math.log(noise_hi)))
    noise = jax.random.normal(key_n, (blocks, BLK, D), jnp.float32) * spread
    return jnp.clip(centres + far_part + noise, -8.0, 8.0).astype(jnp.bfloat16)


def block_sizes(key, blocks):
    key_a, key_b = jax.random.split(key)
    sizes = jax.random.randint(key_a, (blocks,), BLK // 2, BLK + 1, jnp.int32)
    spots = jax.random.permutation(key_b, blocks)
    return sizes.at[spots[0]].set(BLK).at[spots[1]].set(BLK // 2)


def draw_src_points(key, part):
    key = jax.random.fold_in(key, 11)
    return cloud(key, SBLOCKS, 1.5, 0.0, 0.2, 0.3)


def draw_tgt_points(key, part):
    key = jax.random.fold_in(key, 17)
    return cloud(key, TBLOCKS, 1.5, 0.0, 0.2, 0.3)


def draw_src_sizes(key, part):
    key = jax.random.fold_in(key, 23)
    return block_sizes(key, SBLOCKS)


def draw_tgt_sizes(key, part):
    key = jax.random.fold_in(key, 29)
    return block_sizes(key, TBLOCKS)


def free_blocks(shard_key):
    inner = jax.random.permutation(shard_key, TB_DEV - 2) + 1
    lonely = inner[:2]
    block_ids = jnp.arange(TB_DEV, dtype=jnp.int32)
    is_lonely = jnp.any(block_ids[:, None] == lonely[None, :], axis=1).astype(jnp.int32)
    order = jnp.argsort(is_lonely * TB_DEV + block_ids, stable=True)
    return order[:TB_DEV - 2].astype(jnp.int32)


def pick_slots(sub_key):
    return jax.random.permutation(sub_key, TB_DEV - 2)[:KMAX]


def draw_pattern(key, part):
    key = jax.random.fold_in(key, 31)
    shard_keys = jax.random.split(jax.random.fold_in(key, 1), NCOLS)
    usable = jax.vmap(free_blocks)(shard_keys)
    many_keys = jax.random.split(jax.random.fold_in(key, 2), SBLOCKS * NCOLS)
    local_picks = jax.vmap(pick_slots)(many_keys).reshape(SBLOCKS, NCOLS, KMAX).astype(jnp.int32)
    table = jnp.broadcast_to(usable[None, :, :], (SBLOCKS, NCOLS, TB_DEV - 2))
    return jnp.take_along_axis(table, local_picks, axis=2).astype(jnp.int32)


def draw_counts(key, part):
    key = jax.random.fold_in(key, 47)
    key_a, key_b = jax.random.split(key)
    picks = jax.random.randint(key_a, (SBLOCKS * NCOLS,), 1, KMAX + 1, jnp.int32)
    spots = jax.random.permutation(key_b, SBLOCKS * NCOLS)
    picks = picks.at[spots[0]].set(KMAX).at[spots[1]].set(1)
    return picks.reshape(SBLOCKS, NCOLS)


def steps_of(own_key, extent, pieces, low, top_value):
    level = 1.0
    for position, parts in pieces:
        heights = jax.random.uniform(jax.random.fold_in(jax.random.fold_in(own_key, 6), position), (parts,), jnp.float32, low / len(pieces), top_value / len(pieces))
        level = level * jnp.repeat(jnp.exp(heights), extent[position] // parts).reshape((-1,) + (1,) * (len(extent) - 1 - position))
    return level


def setup_inputs(seed: int = 0, part: int = 0) -> dict:
    key_of = jax.random.split(jax.random.key(seed), 9)
    part_splits = jax.random.split(jax.random.fold_in(key_of[8], part), 9)
    src_points = draw_src_points(jax.random.fold_in(jax.random.fold_in(key_of[8], part), 71), part)
    tgt_points = draw_tgt_points(jax.random.fold_in(jax.random.fold_in(key_of[8], part), 71), part)
    src_logw = jnp.clip(jax.random.uniform(part_splits[2], (SBLOCKS, BLK), jnp.float32, -1.0, 1.0) * steps_of(part_splits[2], (SBLOCKS, BLK), ((0, 4),), -0.4, 0.0), -1.0, 1.0)
    tgt_logw = jnp.clip(jax.random.uniform(part_splits[3], (TBLOCKS, BLK), jnp.float32, -1.0, 1.0) * steps_of(part_splits[3], (TBLOCKS, BLK), ((0, 4),), -0.4, 0.0), -1.0, 1.0)
    src_sizes = draw_src_sizes(jax.random.fold_in(jax.random.fold_in(key_of[8], part), 71), part)
    tgt_sizes = draw_tgt_sizes(jax.random.fold_in(jax.random.fold_in(key_of[8], part), 71), part)
    pattern = draw_pattern(jax.random.fold_in(jax.random.fold_in(key_of[8], part), 71), part)
    counts = draw_counts(jax.random.fold_in(jax.random.fold_in(key_of[8], part), 71), part)
    return {"src_points": src_points, "tgt_points": tgt_points, "src_logw": src_logw, "tgt_logw": tgt_logw, "src_sizes": src_sizes, "tgt_sizes": tgt_sizes, "pattern": pattern, "counts": counts}


EPS = 0.5
FLOOR = -1.0e30


def reference(src_points, tgt_points, src_logw, tgt_logw, src_sizes, tgt_sizes, pattern, counts):
    lane_ids = jnp.arange(BLK, dtype=jnp.int32)
    src_valid = lane_ids[None, :] < src_sizes[:, None]
    tgt_valid = lane_ids[None, :] < tgt_sizes[:, None]
    src_norm = jnp.sum(jnp.square(src_points.astype(jnp.float32)), axis=-1)
    tgt_norm = jnp.sum(jnp.square(tgt_points.astype(jnp.float32)), axis=-1)
    shard_base = jnp.arange(NCOLS, dtype=jnp.int32)[:, None] * TB_DEV
    link_ids = (pattern + shard_base[None, :, :]).reshape(SBLOCKS, NCOLS * KMAX).astype(jnp.int32)
    slot_on = (jnp.arange(KMAX, dtype=jnp.int32)[None, None, :] < counts[:, :, None]).reshape(SBLOCKS, NCOLS * KMAX)

    def block_cost(points, point_norm, near_ids):
        near_pts = tgt_points[near_ids].astype(jnp.float32)
        cross_term = jnp.einsum("id,kjd->kij", points.astype(jnp.float32), near_pts)
        return point_norm[None, :, None] + tgt_norm[near_ids][:, None, :] - 2.0 * cross_term

    field_g = jnp.zeros((TBLOCKS, BLK), jnp.float32)
    field_f = jnp.zeros((SBLOCKS, BLK), jnp.float32)
    for repeat in range(ITERS):
        def row_block(scan_item):
            points, point_norm, near_ids, live_slots = scan_item
            pair_cost = block_cost(points, point_norm, near_ids)
            kept_mask = live_slots[:, None, None] & tgt_valid[near_ids][:, None, :]
            scores = jnp.where(kept_mask, (field_g[near_ids][:, None, :] - pair_cost) / EPS, FLOOR)
            row_top = jnp.max(scores, axis=(0, 2))
            row_sum = jnp.sum(jnp.where(kept_mask, jnp.exp(scores - row_top[None, :, None]), 0.0), axis=(0, 2))
            return row_top + jnp.log(row_sum)

        log_sums = lax.map(row_block, (src_points, src_norm, link_ids, slot_on))
        field_f = jnp.where(src_valid, EPS * src_logw - EPS * log_sums, 0.0)

        def col_block(scan_item):
            points, point_norm, near_ids, live_slots, point_valid, src_field = scan_item
            pair_cost = block_cost(points, point_norm, near_ids)
            kept_mask = live_slots[:, None, None] & point_valid[None, :, None] & tgt_valid[near_ids][:, None, :]
            scores = jnp.where(kept_mask, (src_field[None, :, None] - pair_cost) / EPS, FLOOR)
            col_peak = jnp.max(scores, axis=1)
            col_part = jnp.sum(jnp.where(kept_mask, jnp.exp(scores - col_peak[:, None, :]), 0.0), axis=1)
            return col_peak, col_part

        peaks, parts_sum = lax.map(col_block, (src_points, src_norm, link_ids, slot_on, src_valid, field_f))
        flat_ids = link_ids.reshape(-1)
        peaks = peaks.reshape(-1, BLK)
        parts_sum = parts_sum.reshape(-1, BLK)
        col_top = jnp.full((TBLOCKS, BLK), FLOOR, jnp.float32).at[flat_ids].max(peaks)
        col_sum = jnp.zeros((TBLOCKS, BLK), jnp.float32).at[flat_ids].add(parts_sum * jnp.exp(peaks - col_top[flat_ids]))
        reached = tgt_valid & (col_sum >= 0.5)
        field_g = jnp.where(reached, EPS * tgt_logw - EPS * (col_top + jnp.log(jnp.maximum(col_sum, 1.0))), 0.0)
    return field_f, field_g
```

```python
import functools
import math

import jax
import jax.numpy as jnp
from jax import lax
from jax.experimental import pallas as pl
from jax.experimental.pallas import tpu as pltpu
from jax.sharding import PartitionSpec as P

ITERS = 2
EPS = 0.5
LOG2E = math.log2(math.e)
SCALE = 2.0 / EPS * LOG2E
NORM = 1.0 / EPS * LOG2E
FLOOR = -1e30
ABSENT = -1e29
SMALL = 2.0**-80
CHUNK = 8
VMEM_LIMIT = 48 * 1024 * 1024


def transposed_rows(row, size):
    return jnp.broadcast_to(row, (size, row.shape[1])).T


def scores(x_ref, yt_ref, s, t):
    last = yt_ref.shape[0] - 1
    cross = jnp.dot(x_ref[s], yt_ref[jnp.minimum(t, last)], preferred_element_type=jnp.float32)
    return cross * SCALE


def spread(u_ref, ub_ref):
    blocks, size = u_ref.shape

    def body(s, carry):
        ub_ref[s] = transposed_rows(u_ref[pl.ds(s, 1), :], size)
        return carry

    lax.fori_loop(0, blocks, body, 0, unroll=4)


def row_sums(x_ref, yt_ref, u_ref, ub_ref, v_ref, list_s, list_t, chunks, cnt_ref, acc_ref, sum_ref, out_ref):
    blocks, size = u_ref.shape
    acc_ref[...] = jnp.zeros_like(acc_ref)

    def chunk(c, carry):
        for q in range(CHUNK):
            s, t = list_s[c * CHUNK + q], list_t[c * CHUNK + q]
            z = scores(x_ref, yt_ref, s, t) + ub_ref[s] + v_ref[pl.ds(t, 1), :]
            acc_ref[s] += jnp.exp2(z)
        return carry

    lax.fori_loop(0, chunks, chunk, 0)

    def collect(s, carry):
        sum_ref[pl.ds(s, 1), :] = jnp.sum(acc_ref[s].T, axis=0, keepdims=True)
        return carry

    lax.fori_loop(0, blocks, collect, 0, unroll=4)
    total = sum_ref[...]
    u = u_ref[...]
    valid = u > ABSENT
    out_ref[...] = jnp.where(valid, jnp.log2(jnp.maximum(total, SMALL)) - u, FLOOR)
    lowest = jnp.min(jnp.where(valid, total, 1.0))

    @pl.when(lowest < SMALL)
    def _():
        def block(s, first):
            count = cnt_ref[s]

            def raise_top(k, top):
                t = list_t[first + k]
                return jnp.maximum(top, scores(x_ref, yt_ref, s, t) + v_ref[pl.ds(t, 1), :])

            top = lax.fori_loop(0, count, raise_top, jnp.full((size, size), FLOOR, jnp.float32))
            top = jnp.max(top, axis=1, keepdims=True)

            def add(k, acc):
                t = list_t[first + k]
                return acc + jnp.exp2(scores(x_ref, yt_ref, s, t) + v_ref[pl.ds(t, 1), :] - top)

            acc = lax.fori_loop(0, count, add, jnp.zeros((size, size), jnp.float32))
            full = top + jnp.log2(jnp.sum(acc, axis=1, keepdims=True))
            out_ref[pl.ds(s, 1), :] = jnp.broadcast_to(full, (size, size)).T[:1, :]
            return first + count

        lax.fori_loop(0, blocks, block, 0)


def eight(t):
    return pl.ds(pl.multiple_of(t * 8, 8), 8)


def folded(matrix):
    return matrix.reshape(-1, 8, matrix.shape[-1])


def every_eighth(ref, r, count):
    return ref[pl.ds(r, count, stride=8), :]


def col_sums(x_ref, yt_ref, ub_ref, v_ref, touched_ref, list_s, list_t, chunks, acc_ref, top_ref, out_ref):
    targets = yt_ref.shape[0]
    acc_ref[...] = jnp.zeros_like(acc_ref)

    def chunk(c, carry):
        for q in range(CHUNK):
            s, t = list_s[c * CHUNK + q], list_t[c * CHUNK + q]
            z = scores(x_ref, yt_ref, s, t) + ub_ref[s] + v_ref[pl.ds(t, 1), :]
            acc_ref[eight(t), :] += jnp.sum(folded(jnp.exp2(z)), axis=0)
        return carry

    lax.fori_loop(0, chunks, chunk, 0)
    total = sum(every_eighth(acc_ref, r, targets) for r in range(8))
    v = v_ref[:targets, :]
    valid = (v > ABSENT) & (touched_ref[:targets, :] > 0.0)
    out_ref[...] = jnp.where(valid, jnp.log2(jnp.maximum(total, SMALL)) - v, FLOOR)
    lowest = jnp.min(jnp.where(valid, total, 1.0))

    @pl.when(lowest < SMALL)
    def _():
        acc_ref[...] = jnp.zeros_like(acc_ref)
        top_ref[...] = jnp.full_like(top_ref, FLOOR)

        def raise_top(p, carry):
            s, t = list_s[p], list_t[p]
            z = scores(x_ref, yt_ref, s, t) + ub_ref[s]
            top_ref[eight(t), :] = jnp.maximum(top_ref[eight(t), :], jnp.max(folded(z), axis=0))
            return carry

        lax.fori_loop(0, chunks * CHUNK, raise_top, 0)
        tops = [every_eighth(top_ref, r, targets) for r in range(8)]
        top = functools.reduce(jnp.maximum, tops)
        out_ref[...] = top

        def add(p, carry):
            s, t = list_s[p], list_t[p]
            peak = out_ref[pl.ds(jnp.minimum(t, targets - 1), 1), :]
            z = scores(x_ref, yt_ref, s, t) + ub_ref[s] - peak
            acc_ref[eight(t), :] += jnp.sum(folded(jnp.exp2(jnp.minimum(z, 0.0))), axis=0)
            return carry

        lax.fori_loop(0, chunks * CHUNK, add, 0)
        exact = sum(every_eighth(acc_ref, r, targets) for r in range(8))
        out_ref[...] = jnp.where(valid, top + jnp.log2(jnp.maximum(exact, 1.0)), FLOOR)


def merged(parts):
    top = functools.reduce(jnp.maximum, parts)
    return top, top + jnp.log2(sum(jnp.exp2(part - top) for part in parts))


def first_kernel(
    ssz_ref, tsz_ref, pat_ref, cnt_ref, xt_ref, yt_ref,
    x_ref, u_ref, v_ref, touched_ref, list_s, list_t, chunks_ref, out_ref,
    ub_ref, acc_ref, sum_ref,
):
    blocks, size = u_ref.shape
    targets = yt_ref.shape[0]
    slots = pat_ref.shape[0]
    lanes = lax.broadcasted_iota(jnp.int32, (1, size), 1)

    def list_block(s, p):
        count = cnt_ref[s]
        for k in range(slots):
            list_s[p] = s
            list_t[p] = pat_ref[k, s]
            p = p + (k < count).astype(jnp.int32)
        return p

    pairs = lax.fori_loop(0, blocks, list_block, 0)
    for q in range(CHUNK):
        list_s[pairs + q] = blocks - 1
        list_t[pairs + q] = targets
    chunks = (pairs + CHUNK - 1) // CHUNK
    chunks_ref[0] = chunks

    def source(s, carry):
        xt = xt_ref[s].astype(jnp.float32)
        x_ref[s] = xt.T.astype(jnp.bfloat16)
        u = -NORM * jnp.sum(xt * xt, axis=0, keepdims=True)
        u_ref[pl.ds(s, 1), :] = jnp.where(lanes < ssz_ref[s], u, FLOOR)
        return carry

    lax.fori_loop(0, blocks, source, 0, unroll=4)
    v_ref[pl.ds(targets, v_ref.shape[0] - targets), :] = jnp.full(
        (v_ref.shape[0] - targets, size), FLOOR, jnp.float32
    )

    def target(t, carry):
        yt = yt_ref[t].astype(jnp.float32)
        v = -NORM * jnp.sum(yt * yt, axis=0, keepdims=True)
        v_ref[pl.ds(t, 1), :] = jnp.where(lanes < tsz_ref[t], v, FLOOR)
        return carry

    lax.fori_loop(0, targets, target, 0, unroll=8)
    touched_ref[...] = jnp.zeros_like(touched_ref)

    def touch(p, carry):
        touched_ref[pl.ds(list_t[p], 1), :] = jnp.ones((1, size), jnp.float32)
        return carry

    lax.fori_loop(0, chunks * CHUNK, touch, 0)
    spread(u_ref, ub_ref)
    row_sums(x_ref, yt_ref, u_ref, ub_ref, v_ref, list_s, list_t, chunks, cnt_ref, acc_ref, sum_ref, out_ref)


def col_kernel(
    n_parts, last, list_s, list_t, chunks_ref, x_ref, yt_ref, u0_ref, v_ref, touched_ref, logw_ref, *rest
):
    parts, (u_ref, out_ref, ub_ref, acc_ref, top_ref) = rest[:n_parts], rest[n_parts:]
    u0 = u0_ref[...]
    valid = u0 > ABSENT
    _, total = merged([part[...] for part in parts])
    u = jnp.where(valid, LOG2E * logw_ref[...] - total, FLOOR)
    u_ref[...] = u
    spread(u_ref, ub_ref)
    col_sums(x_ref, yt_ref, ub_ref, v_ref, touched_ref, list_s, list_t, chunks_ref[0], acc_ref, top_ref, out_ref)
    if last:
        u_ref[...] = jnp.where(valid, (u - u0) / NORM, 0.0)


def row_kernel(
    n_parts, list_s, list_t, chunks_ref, cnt_ref, x_ref, yt_ref, u_ref, v0_ref, logw_ref, *rest
):
    parts, (v_ref, out_ref, ub_ref, acc_ref, sum_ref) = rest[:n_parts], rest[n_parts:]
    targets = yt_ref.shape[0]
    top, total = merged([part[...] for part in parts])
    valid = (v0_ref[:targets, :] > ABSENT) & (top > ABSENT)
    v_ref[...] = v0_ref[...]
    v_ref[:targets, :] = jnp.where(valid, LOG2E * logw_ref[...] - total, v0_ref[:targets, :])
    spread(u_ref, ub_ref)
    row_sums(x_ref, yt_ref, u_ref, ub_ref, v_ref, list_s, list_t, chunks_ref[0], cnt_ref, acc_ref, sum_ref, out_ref)


def last_kernel(n_parts, v0_ref, logw_ref, *rest):
    parts, (out_ref,) = rest[:n_parts], rest[n_parts:]
    targets = logw_ref.shape[0]
    top, total = merged([part[...] for part in parts])
    v0 = v0_ref[:targets, :]
    valid = (v0 > ABSENT) & (top > ABSENT)
    out_ref[...] = jnp.where(valid, (LOG2E * logw_ref[...] - total - v0) / NORM, 0.0)


def call(kernel, outs, scratch, spaces_in, spaces_out, *args):
    where = {"v": pltpu.VMEM, "s": pltpu.SMEM}
    return pl.pallas_call(
        kernel,
        out_shape=outs,
        in_specs=[pl.BlockSpec(memory_space=where[k]) for k in spaces_in],
        out_specs=[pl.BlockSpec(memory_space=where[k]) for k in spaces_out],
        scratch_shapes=scratch,
        compiler_params=pltpu.CompilerParams(vmem_limit_bytes=VMEM_LIMIT),
    )(*args)


def exchanged(part, axis):
    size = lax.axis_size(axis)
    pieces = [part]
    for d in range(1, size):
        if size & (size - 1):
            pairs = [(i, (i + d) % size) for i in range(size)]
        else:
            pairs = [(i, i ^ d) for i in range(size)]
        pieces.append(lax.ppermute(part, axis, pairs))
    return pieces


def on_device(src_points, tgt_points, src_logw, tgt_logw, src_sizes, tgt_sizes, pattern, counts):
    blocks, size, dims = src_points.shape
    targets = tgt_points.shape[0]
    slots = pattern.shape[2]
    f32, i32 = jnp.float32, jnp.int32
    xt = jnp.swapaxes(src_points, 1, 2)
    yt = jnp.swapaxes(tgt_points, 1, 2)
    pat = pattern[:, 0, :].T
    cnt = counts[:, 0]
    room = blocks * slots + 2 * CHUNK
    struct = jax.ShapeDtypeStruct
    ub = pltpu.VMEM((blocks, size, size), f32)
    acc_row = pltpu.VMEM((blocks, size, size), f32)
    sums = pltpu.VMEM((blocks, size), f32)
    acc_col = pltpu.VMEM(((targets + 8) * 8, size), f32)

    x, u0, v0, touched, list_s, list_t, chunks, row_part = call(
        first_kernel,
        [
            struct((blocks, size, dims), jnp.bfloat16),
            struct((blocks, size), f32),
            struct((targets + 8, size), f32),
            struct((targets + 8, size), f32),
            struct((room,), i32),
            struct((room,), i32),
            struct((1,), i32),
            struct((blocks, size), f32),
        ],
        [ub, acc_row, sums],
        "ssssvv",
        "vvvvsssv",
        src_sizes, tgt_sizes, pat, cnt, xt, yt,
    )
    v = v0
    for repeat in range(ITERS):
        row_parts = exchanged(row_part, "col")
        u, col_part = call(
            functools.partial(col_kernel, len(row_parts), repeat == ITERS - 1),
            [struct((blocks, size), f32), struct((targets, size), f32)],
            [ub, acc_col, acc_col],
            "sss" + "v" * (6 + len(row_parts)),
            "vv",
            list_s, list_t, chunks, x, yt, u0, v, touched, src_logw, *row_parts,
        )
        col_parts = exchanged(col_part, "row")
        if repeat < ITERS - 1:
            v, row_part = call(
                functools.partial(row_kernel, len(col_parts)),
                [struct((targets + 8, size), f32), struct((blocks, size), f32)],
                [ub, acc_row, sums],
                "ssss" + "v" * (5 + len(col_parts)),
                "vv",
                list_s, list_t, chunks, cnt, x, yt, u, v0, tgt_logw, *col_parts,
            )
    (field_g,) = call(
        functools.partial(last_kernel, len(col_parts)),
        [struct((targets, size), f32)],
        [],
        "v" * (2 + len(col_parts)),
        "v",
        v0, tgt_logw, *col_parts,
    )
    return u, field_g


def solution(mesh):
    return jax.shard_map(
        on_device,
        mesh=mesh,
        in_specs=(
            P(("groups", "row"), None, None),
            P(("groups", "col"), None, None),
            P(("groups", "row"), None),
            P(("groups", "col"), None),
            P(("groups", "row")),
            P(("groups", "col")),
            P(("groups", "row"), "col", None),
            P(("groups", "row"), "col"),
        ),
        out_specs=(P(("groups", "row"), None), P(("groups", "col"), None)),
        check_vma=False,
    )
```

```python
import functools
import math

import jax
import jax.numpy as jnp
from jax import lax
from jax.experimental import pallas as pl
from jax.experimental.pallas import tpu as pltpu
from jax.sharding import PartitionSpec as P

ITERS = 2
EPS = 0.5
LOG2E = math.log2(math.e)
SCALE = 2.0 / EPS * LOG2E
FIELD = EPS / LOG2E
FLOOR = -1e30
ABSENT = -1e29
SMALL = 2.0**-80
CHUNK = 16
EXTRA = 16
VMEM_LIMIT = 26 * 1024 * 1024


def eight(t):
    return pl.ds(pl.multiple_of(t * 8, 8), 8)


def folded(matrix):
    return matrix.reshape(-1, 8, matrix.shape[-1])


def every_eighth(ref, r, count):
    return ref[pl.ds(r, count, stride=8), :]


def merged(parts):
    top = functools.reduce(jnp.maximum, parts)
    total = top + jnp.log2(sum(jnp.exp2(part - top) for part in parts))
    return top > ABSENT, total


def spread(p_ref, pb_ref):
    blocks, size = p_ref.shape

    def body(s, carry):
        pb_ref[s] = jnp.broadcast_to(p_ref[pl.ds(s, 1), :], (size, size)).T
        return carry

    lax.fori_loop(0, blocks, body, 0, unroll=16)


def collect(acc_ref, sum_ref):
    def body(s, carry):
        sum_ref[pl.ds(s, 1), :] = jnp.sum(acc_ref[s].T, axis=0, keepdims=True)
        return carry

    lax.fori_loop(0, acc_ref.shape[0], body, 0, unroll=16)


def row_result(total, shift, valid, z_ref, q_ref, lists, pairs, out_ref):
    blocks, size = out_ref.shape
    out_ref[...] = jnp.where(valid, jnp.log2(jnp.maximum(total, SMALL)) - shift, FLOOR)
    lowest = jnp.min(jnp.where(valid, total, 1.0))

    @pl.when(lowest < SMALL)
    def _():
        def score(p):
            z = z_ref[p]
            return z if q_ref is None else z + q_ref[pl.ds(lists[lists.shape[0] // 2 + p], 1), :]

        def block(s, first):
            def same(p):
                return (p < pairs) & (lists[jnp.minimum(p, pairs - 1)] == s)

            def raise_top(carry):
                return carry[0] + 1, jnp.maximum(carry[1], score(carry[0]))

            start = (first, jnp.full((size, size), 2.0 * FLOOR, jnp.float32))
            end, top = lax.while_loop(lambda carry: same(carry[0]), raise_top, start)
            top = jnp.max(top, axis=1, keepdims=True)

            def add(p, acc):
                return acc + jnp.exp2(score(p) - top)

            acc = lax.fori_loop(first, end, add, jnp.zeros((size, size), jnp.float32))
            full = top + jnp.log2(jnp.sum(acc, axis=1, keepdims=True))
            out_ref[pl.ds(s, 1), :] = jnp.broadcast_to(full, (size, size)).T[:1, :]
            return end

        lax.fori_loop(0, blocks, block, 0)
        out_ref[...] = jnp.where(valid, out_ref[...], FLOOR)


def col_pass(z_ref, pb_ref, q_ref, touched_ref, lists, pairs, acc_ref, top_ref, out_ref):
    targets = out_ref.shape[0]
    room = lists.shape[0] // 2
    acc_ref[...] = jnp.zeros_like(acc_ref)

    def chunk(c, carry):
        for k in range(CHUNK):
            s, t = lists[c * CHUNK + k], lists[room + c * CHUNK + k]
            z = z_ref[c * CHUNK + k] + pb_ref[s]
            if q_ref is not None:
                z = z + q_ref[pl.ds(t, 1), :]
            acc_ref[eight(t), :] += jnp.sum(folded(jnp.exp2(z)), axis=0)
        return carry

    lax.fori_loop(0, (pairs + CHUNK - 1) // CHUNK, chunk, 0)
    total = sum(every_eighth(acc_ref, r, targets) for r in range(8))
    valid = touched_ref[:targets, :] > 0.0
    shift = 0.0 if q_ref is None else q_ref[:targets, :]
    out_ref[...] = jnp.where(valid, jnp.log2(jnp.maximum(total, SMALL)) - shift, FLOOR)
    lowest = jnp.min(jnp.where(valid, total, 1.0))

    @pl.when(lowest < SMALL)
    def _():
        acc_ref[...] = jnp.zeros_like(acc_ref)
        top_ref[...] = jnp.full_like(top_ref, 2.0 * FLOOR)

        def raise_top(p, carry):
            s, t = lists[p], lists[room + p]
            z = z_ref[p] + pb_ref[s]
            top_ref[eight(t), :] = jnp.maximum(top_ref[eight(t), :], jnp.max(folded(z), axis=0))
            return carry

        lax.fori_loop(0, pairs, raise_top, 0)
        top = functools.reduce(jnp.maximum, [every_eighth(top_ref, r, targets) for r in range(8)])
        out_ref[...] = top

        def add(p, carry):
            s, t = lists[p], lists[room + p]
            z = z_ref[p] + pb_ref[s] - out_ref[pl.ds(t, 1), :]
            acc_ref[eight(t), :] += jnp.sum(folded(jnp.exp2(z)), axis=0)
            return carry

        lax.fori_loop(0, pairs, add, 0)
        exact = sum(every_eighth(acc_ref, r, targets) for r in range(8))
        out_ref[...] = jnp.where(valid, top + jnp.log2(jnp.maximum(exact, 1.0)), FLOOR)


def three_terms(row):
    high = row.astype(jnp.bfloat16)
    rest = row - high.astype(jnp.float32)
    middle = rest.astype(jnp.bfloat16)
    low = (rest - middle.astype(jnp.float32)).astype(jnp.bfloat16)
    return [high.astype(jnp.float32), middle.astype(jnp.float32), low.astype(jnp.float32)]


def extra_rows(row, first, width):
    place = lax.broadcasted_iota(jnp.int32, (EXTRA, width), 0)
    result = jnp.where((place < 6) & ((place < first) | (place >= first + 3)), 1.0, 0.0)
    for k, term in enumerate(three_terms(row)):
        result = jnp.where(place == first + k, term, result)
    return result.astype(jnp.bfloat16)


def first_kernel(
    ssz_any, tsz_any, pat_any, cnt_any, xt_any, yt_any,
    z_ref, touched_ref, lists_ref, out_ref,
    ssz_ref, tsz_ref, pat_ref, cnt_ref, lists_smem, xt_ref, x_ref, y_ref, mask_ref, live_ref, acc_ref, sum_ref, sems,
):
    blocks, size = out_ref.shape
    dims = xt_ref.shape[1]
    targets = yt_any.shape[0]
    slots = pat_ref.shape[0]
    room = lists_smem.shape[0] // 2
    small = [
        pltpu.make_async_copy(source, target, sems.at[k])
        for k, (source, target) in enumerate(
            [(ssz_any, ssz_ref), (tsz_any, tsz_ref), (pat_any, pat_ref), (cnt_any, cnt_ref)]
        )
    ]
    copy_x = pltpu.make_async_copy(xt_any, xt_ref, sems.at[4])
    copy_y = pltpu.make_async_copy(yt_any, y_ref.at[pl.ds(0, targets), pl.ds(0, dims), :], sems.at[5])
    for copy in small:
        copy.start()
    copy_x.start()
    copy_y.start()
    acc_ref[...] = jnp.zeros_like(acc_ref)
    touched_ref[...] = jnp.zeros_like(touched_ref)
    y_ref[targets] = jnp.zeros(y_ref.shape[1:], jnp.bfloat16)
    mask_ref[pl.ds(targets, 8), :] = jnp.zeros((8, size), jnp.float32)
    lanes = lax.broadcasted_iota(jnp.int32, (1, size), 1)
    y_ref[targets, pl.ds(dims, EXTRA), :] = extra_rows(jnp.full((1, size), FLOOR, jnp.float32), 3, size)
    for copy in small:
        copy.wait()

    def list_block(s, p):
        count = cnt_ref[s]
        for k in range(slots):
            lists_smem[p] = s
            lists_smem[room + p] = pat_ref[k, s]
            p = p + (k < count).astype(jnp.int32)
        return p

    pairs = lax.fori_loop(0, blocks, list_block, 0)
    for k in range(CHUNK):
        lists_smem[pairs + k] = blocks - 1
        lists_smem[room + pairs + k] = targets
    lists_smem[room - 1] = pairs
    copy_lists = pltpu.make_async_copy(lists_smem, lists_ref, sems.at[6])
    copy_lists.start()
    copy_x.wait()

    def source(s, carry):
        xt = xt_ref[s].astype(jnp.float32)
        live = lanes < ssz_ref[s]
        norm = jnp.where(live, -0.5 * jnp.sum(xt * xt, axis=0, keepdims=True), FLOOR)
        live_ref[pl.ds(s, 1), :] = live.astype(jnp.float32)
        extra = extra_rows(norm, 0, size).astype(jnp.float32)
        x_ref[s] = jnp.concatenate([xt, extra], axis=0).T.astype(jnp.bfloat16)
        return carry

    lax.fori_loop(0, blocks, source, 0, unroll=4)
    copy_y.wait()

    def target(t, carry):
        yt = y_ref[t, pl.ds(0, dims), :].astype(jnp.float32)
        live = lanes < tsz_ref[t]
        norm = jnp.where(live, -0.5 * jnp.sum(yt * yt, axis=0, keepdims=True), FLOOR)
        mask_ref[pl.ds(t, 1), :] = live.astype(jnp.float32)
        y_ref[t, pl.ds(dims, EXTRA), :] = extra_rows(norm, 3, size)
        return carry

    lax.fori_loop(0, targets, target, 0, unroll=8)

    def chunk(c, carry):
        for k in range(CHUNK):
            s, t = lists_smem[c * CHUNK + k], lists_smem[room + c * CHUNK + k]
            z = jnp.dot(x_ref[s], y_ref[t], preferred_element_type=jnp.float32) * SCALE
            z_ref[c * CHUNK + k] = z
            acc_ref[s] += jnp.exp2(z)
            touched_ref[pl.ds(t, 1), :] = mask_ref[pl.ds(t, 1), :]
        return carry

    lax.fori_loop(0, (pairs + CHUNK - 1) // CHUNK, chunk, 0)
    collect(acc_ref, sum_ref)
    valid = live_ref[...] > 0.0
    row_result(sum_ref[...], 0.0, valid, z_ref, None, lists_smem, pairs, out_ref)
    copy_lists.wait()


def col_kernel(n_parts, has_q, last, lists_ref, z_ref, touched_ref, logw_ref, *rest):
    q_ref, rest = (rest[0], rest[1:]) if has_q else (None, rest)
    parts, rest = rest[:n_parts], rest[n_parts:]
    p_ref, out_ref, pb_ref, lists_smem, acc_ref, top_ref, sem = rest
    copy = pltpu.make_async_copy(lists_ref, lists_smem, sem)
    copy.start()
    valid, total = merged([part[...] for part in parts])
    p_ref[...] = jnp.where(valid, LOG2E * logw_ref[...] - total, 0.0)
    spread(p_ref, pb_ref)
    copy.wait()
    room = lists_smem.shape[0] // 2
    col_pass(
        z_ref, pb_ref, q_ref, touched_ref, lists_smem, lists_smem[room - 1], acc_ref, top_ref, out_ref
    )
    if last:
        p_ref[...] = p_ref[...] * FIELD


def row_kernel(n_parts, lists_ref, z_ref, p_ref, pb_ref, earlier_ref, logw_ref, *rest):
    parts, (q_ref, out_ref, lists_smem, acc_ref, sum_ref, sem) = rest[:n_parts], rest[n_parts:]
    targets = logw_ref.shape[0]
    copy = pltpu.make_async_copy(lists_ref, lists_smem, sem)
    copy.start()
    valid, total = merged([part[...] for part in parts])
    q_ref[pl.ds(0, targets), :] = jnp.where(valid, LOG2E * logw_ref[...] - total, 0.0)
    q_ref[pl.ds(targets, 8), :] = jnp.zeros((8, q_ref.shape[1]), jnp.float32)
    acc_ref[...] = jnp.zeros_like(acc_ref)
    copy.wait()
    room = lists_smem.shape[0] // 2
    pairs = lists_smem[room - 1]

    def chunk(c, carry):
        for k in range(CHUNK):
            s, t = lists_smem[c * CHUNK + k], lists_smem[room + c * CHUNK + k]
            acc_ref[s] += jnp.exp2(z_ref[c * CHUNK + k] + pb_ref[s] + q_ref[pl.ds(t, 1), :])
        return carry

    lax.fori_loop(0, (pairs + CHUNK - 1) // CHUNK, chunk, 0)
    collect(acc_ref, sum_ref)
    row_result(
        sum_ref[...], p_ref[...], earlier_ref[...] > ABSENT, z_ref, q_ref,
        lists_smem, pairs, out_ref,
    )


def last_kernel(n_parts, logw_ref, *rest):
    parts, (out_ref,) = rest[:n_parts], rest[n_parts:]
    valid, total = merged([part[...] for part in parts])
    out_ref[...] = jnp.where(valid, (LOG2E * logw_ref[...] - total) * FIELD, 0.0)


def call(kernel, name, outs, scratch, args, spaces="v"):
    where = {"v": pltpu.VMEM, "h": pltpu.HBM}
    return pl.pallas_call(
        kernel,
        out_shape=outs,
        in_specs=[pl.BlockSpec(memory_space=where[k]) for k in (spaces * len(args))[: len(args)]],
        out_specs=[pl.BlockSpec(memory_space=pltpu.VMEM)] * len(outs),
        scratch_shapes=scratch,
        name=name,
        compiler_params=pltpu.CompilerParams(vmem_limit_bytes=VMEM_LIMIT),
    )(*args)


def exchanged(part, axis):
    size = lax.axis_size(axis)
    pieces = [part]
    for d in range(1, size):
        if size & (size - 1):
            pairs = [(i, (i + d) % size) for i in range(size)]
        else:
            pairs = [(i, i ^ d) for i in range(size)]
        pieces.append(lax.ppermute(part, axis, pairs))
    return pieces


def on_device(src_points, tgt_points, src_logw, tgt_logw, src_sizes, tgt_sizes, pattern, counts):
    blocks, size, dims = src_points.shape
    targets = tgt_points.shape[0]
    slots = pattern.shape[2]
    f32, i32, bf16 = jnp.float32, jnp.int32, jnp.bfloat16
    xt = jnp.swapaxes(src_points, 1, 2)
    yt = jnp.swapaxes(tgt_points, 1, 2)
    room = -(-(blocks * slots + CHUNK + 1) // 512) * 512
    struct = jax.ShapeDtypeStruct
    dma = pltpu.SemaphoreType.DMA
    wide = pltpu.VMEM((blocks, size, size), f32)
    sums = pltpu.VMEM((blocks, size), f32)
    acc_col = pltpu.VMEM(((targets + 8) * 8, size), f32)
    lists_smem = pltpu.SMEM((2 * room,), i32)

    z, touched, lists, row_part = call(
        first_kernel,
        "scores_and_rows",
        [
            struct((blocks * slots + CHUNK, size, size), f32),
            struct((targets + 8, size), f32),
            struct((2 * room,), i32),
            struct((blocks, size), f32),
        ],
        [
            pltpu.SMEM((blocks,), i32),
            pltpu.SMEM((targets,), i32),
            pltpu.SMEM((slots, blocks), i32),
            pltpu.SMEM((blocks,), i32),
            lists_smem,
            pltpu.VMEM((blocks, dims, size), bf16),
            pltpu.VMEM((blocks, size, dims + EXTRA), bf16),
            pltpu.VMEM((targets + 1, dims + EXTRA, size), bf16),
            pltpu.VMEM((targets + 8, size), f32),
            sums,
            wide,
            sums,
            dma((7,)),
        ],
        [src_sizes, tgt_sizes, pattern[:, 0, :].T, counts[:, 0], xt, yt],
        "h",
    )
    first_part = row_part
    q = None
    for repeat in range(ITERS):
        last = repeat == ITERS - 1
        row_parts = exchanged(row_part, "col")
        results = call(
            functools.partial(col_kernel, len(row_parts), q is not None, last),
            "columns",
            [struct((blocks, size), f32), struct((targets, size), f32)]
            + ([] if last else [struct((blocks, size, size), f32)]),
            ([wide] if last else []) + [lists_smem, acc_col, acc_col, dma],
            [lists, z, touched, src_logw] + ([] if q is None else [q]) + row_parts,
        )
        p, col_part, *pb = results
        col_parts = exchanged(col_part, "row")
        if not last:
            q, row_part = call(
                functools.partial(row_kernel, len(col_parts)),
                "rows",
                [struct((targets + 8, size), f32), struct((blocks, size), f32)],
                [lists_smem, wide, sums, dma],
                [lists, z, p, *pb, first_part, tgt_logw] + col_parts,
            )
    (field_g,) = call(
        functools.partial(last_kernel, len(col_parts)),
        "target_field",
        [struct((targets, size), f32)],
        [],
        [tgt_logw] + col_parts,
    )
    return p, field_g


def solution(mesh):
    return jax.shard_map(
        on_device,
        mesh=mesh,
        in_specs=(
            P(("groups", "row"), None, None),
            P(("groups", "col"), None, None),
            P(("groups", "row"), None),
            P(("groups", "col"), None),
            P(("groups", "row")),
            P(("groups", "col")),
            P(("groups", "row"), "col", None),
            P(("groups", "row"), "col"),
        ),
        out_specs=(P(("groups", "row"), None), P(("groups", "col"), None)),
        check_vma=False,
    )
```

```python
import functools
import math

import jax
import jax.numpy as jnp
from jax import lax
from jax.experimental import pallas as pl
from jax.experimental.pallas import tpu as pltpu
from jax.sharding import PartitionSpec as P

ITERS = 2
EPS = 0.5
LOG2E = math.log2(math.e)
SCALE = 2.0 / EPS * LOG2E
FIELD = EPS / LOG2E
FLOOR = -1e30
ABSENT = -1e29
SMALL = 2.0**-80
CHUNK = 16
LARGE_CHUNK = 64
EXTRA = 16
VMEM_LIMIT = 26 * 1024 * 1024


def eight(t):
    return pl.ds(pl.multiple_of(t * 8, 8), 8)


def folded(matrix):
    return matrix.reshape(-1, 8, matrix.shape[-1])


def every_eighth(ref, r, count):
    return ref[pl.ds(r, count, stride=8), :]


def merged(parts):
    top = functools.reduce(jnp.maximum, parts)
    total = top + jnp.log2(sum(jnp.exp2(part - top) for part in parts))
    return top > ABSENT, total


def spread(p_ref, pb_ref):
    blocks, size = p_ref.shape

    def body(s, carry):
        pb_ref[s] = jnp.broadcast_to(p_ref[pl.ds(s, 1), :], (size, size)).T
        return carry

    lax.fori_loop(0, blocks, body, 0, unroll=16)


def collect(acc_ref, sum_ref):
    def body(s, carry):
        sum_ref[pl.ds(s, 1), :] = jnp.sum(acc_ref[s].T, axis=0, keepdims=True)
        return carry

    lax.fori_loop(0, acc_ref.shape[0], body, 0, unroll=16)


def row_result(total, shift, valid, z_ref, q_ref, lists, pairs, out_ref):
    blocks, size = out_ref.shape
    out_ref[...] = jnp.where(valid, jnp.log2(jnp.maximum(total, SMALL)) - shift, FLOOR)
    lowest = jnp.min(jnp.where(valid, total, 1.0))

    @pl.when(lowest < SMALL)
    def _():
        def score(p):
            z = z_ref[p]
            return z if q_ref is None else z + q_ref[pl.ds(lists[lists.shape[0] // 2 + p], 1), :]

        def block(s, first):
            def same(p):
                return (p < pairs) & (lists[jnp.minimum(p, pairs - 1)] == s)

            def raise_top(carry):
                return carry[0] + 1, jnp.maximum(carry[1], score(carry[0]))

            start = (first, jnp.full((size, size), 2.0 * FLOOR, jnp.float32))
            end, top = lax.while_loop(lambda carry: same(carry[0]), raise_top, start)
            top = jnp.max(top, axis=1, keepdims=True)

            def add(p, acc):
                return acc + jnp.exp2(score(p) - top)

            acc = lax.fori_loop(first, end, add, jnp.zeros((size, size), jnp.float32))
            full = top + jnp.log2(jnp.sum(acc, axis=1, keepdims=True))
            out_ref[pl.ds(s, 1), :] = jnp.broadcast_to(full, (size, size)).T[:1, :]
            return end

        lax.fori_loop(0, blocks, block, 0)
        out_ref[...] = jnp.where(valid, out_ref[...], FLOOR)


def col_pass(z_ref, pb_ref, q_ref, touched_ref, lists, pairs, acc_ref, top_ref, out_ref):
    targets = out_ref.shape[0]
    room = lists.shape[0] // 2
    acc_ref[...] = jnp.zeros_like(acc_ref)

    def chunk(c, carry):
        for k in range(CHUNK):
            s, t = lists[c * CHUNK + k], lists[room + c * CHUNK + k]
            z = z_ref[c * CHUNK + k] + pb_ref[s]
            if q_ref is not None:
                z = z + q_ref[pl.ds(t, 1), :]
            acc_ref[eight(t), :] += jnp.sum(folded(jnp.exp2(z)), axis=0)
        return carry

    lax.fori_loop(0, (pairs + CHUNK - 1) // CHUNK, chunk, 0)
    total = sum(every_eighth(acc_ref, r, targets) for r in range(8))
    valid = touched_ref[:targets, :] > 0.0
    shift = 0.0 if q_ref is None else q_ref[:targets, :]
    out_ref[...] = jnp.where(valid, jnp.log2(jnp.maximum(total, SMALL)) - shift, FLOOR)
    lowest = jnp.min(jnp.where(valid, total, 1.0))

    @pl.when(lowest < SMALL)
    def _():
        acc_ref[...] = jnp.zeros_like(acc_ref)
        top_ref[...] = jnp.full_like(top_ref, 2.0 * FLOOR)

        def raise_top(p, carry):
            s, t = lists[p], lists[room + p]
            z = z_ref[p] + pb_ref[s]
            top_ref[eight(t), :] = jnp.maximum(top_ref[eight(t), :], jnp.max(folded(z), axis=0))
            return carry

        lax.fori_loop(0, pairs, raise_top, 0)
        top = functools.reduce(jnp.maximum, [every_eighth(top_ref, r, targets) for r in range(8)])
        out_ref[...] = top

        def add(p, carry):
            s, t = lists[p], lists[room + p]
            z = z_ref[p] + pb_ref[s] - out_ref[pl.ds(t, 1), :]
            acc_ref[eight(t), :] += jnp.sum(folded(jnp.exp2(z)), axis=0)
            return carry

        lax.fori_loop(0, pairs, add, 0)
        exact = sum(every_eighth(acc_ref, r, targets) for r in range(8))
        out_ref[...] = jnp.where(valid, top + jnp.log2(jnp.maximum(exact, 1.0)), FLOOR)


def three_terms(row):
    high = row.astype(jnp.bfloat16)
    rest = row - high.astype(jnp.float32)
    middle = rest.astype(jnp.bfloat16)
    low = (rest - middle.astype(jnp.float32)).astype(jnp.bfloat16)
    return [high.astype(jnp.float32), middle.astype(jnp.float32), low.astype(jnp.float32)]


def extra_rows(row):
    place = lax.broadcasted_iota(jnp.int32, (EXTRA, row.shape[1]), 0)
    result = jnp.zeros(place.shape, jnp.float32)
    for k, term in enumerate(three_terms(row)):
        result = jnp.where(place == k, term, result)
    return result


def first_kernel(
    ssz_any, tsz_any, pat_any, cnt_any, xt_any, yt_any,
    z_ref, touched_ref, lists_ref, out_ref,
    ssz_ref, tsz_ref, pat_ref, cnt_ref, lists_smem, xt_ref, x_ref, y_ref, norm_ref, part_ref, live_ref, acc_ref, sum_ref,
    sems,
):
    blocks, size = out_ref.shape
    dims = xt_ref.shape[1]
    targets = yt_any.shape[0]
    slots = pat_ref.shape[0]
    room = lists_smem.shape[0] // 2
    small = [
        pltpu.make_async_copy(source, target, sems.at[k])
        for k, (source, target) in enumerate(
            [(ssz_any, ssz_ref), (tsz_any, tsz_ref), (pat_any, pat_ref), (cnt_any, cnt_ref)]
        )
    ]
    copy_x = pltpu.make_async_copy(xt_any, xt_ref, sems.at[4])
    copy_y = pltpu.make_async_copy(yt_any, y_ref.at[pl.ds(0, targets), pl.ds(0, dims), :], sems.at[5])
    for copy in small:
        copy.start()
    copy_x.start()
    copy_y.start()
    acc_ref[...] = jnp.zeros_like(acc_ref)
    touched_ref[...] = jnp.zeros_like(touched_ref)
    lanes = lax.broadcasted_iota(jnp.int32, (1, size), 1)
    ones = (lax.broadcasted_iota(jnp.int32, (EXTRA, size), 0) < 3).astype(jnp.bfloat16)

    def pad_rows(t, carry):
        y_ref[t, pl.ds(dims, EXTRA), :] = ones
        return carry

    lax.fori_loop(0, targets, pad_rows, 0, unroll=16)
    y_ref[targets] = jnp.zeros(y_ref.shape[1:], jnp.bfloat16)
    norm_ref[pl.ds(targets, 8), :] = jnp.full((8, size), FLOOR, jnp.float32)
    for copy in small:
        copy.wait()
    copy_x.wait()

    def source(s, p):
        xt = xt_ref[s].astype(jnp.float32)
        live = lanes < ssz_ref[s]
        norm = jnp.where(live, -0.5 * jnp.sum(xt * xt, axis=0, keepdims=True), FLOOR)
        live_ref[pl.ds(s, 1), :] = live.astype(jnp.float32)
        x_ref[s] = jnp.concatenate([xt, extra_rows(norm)], axis=0).T.astype(jnp.bfloat16)
        count = cnt_ref[s]
        for k in range(slots):
            lists_smem[p] = s
            lists_smem[room + p] = pat_ref[k, s]
            p = p + (k < count).astype(jnp.int32)
        return p

    pairs = lax.fori_loop(0, blocks, source, 0, unroll=8)
    for k in range(CHUNK):
        lists_smem[pairs + k] = blocks - 1
        lists_smem[room + pairs + k] = targets
    lists_smem[room - 1] = pairs
    copy_lists = pltpu.make_async_copy(lists_smem, lists_ref, sems.at[6])
    copy_lists.start()
    copy_y.wait()

    def target(t, carry):
        yt = y_ref[t, pl.ds(0, dims), :].astype(jnp.float32)
        part_ref[eight(t), :] = jnp.sum(folded(yt * yt), axis=0)
        return carry

    lax.fori_loop(0, targets, target, 0, unroll=16)
    sizes = jnp.broadcast_to(tsz_ref[...].astype(jnp.float32), (size, targets)).T
    mask = lax.broadcasted_iota(jnp.int32, (targets, size), 1).astype(jnp.float32) < sizes
    norms = sum(every_eighth(part_ref, r, targets) for r in range(8))
    norm_ref[pl.ds(0, targets), :] = jnp.where(mask, (-0.5 * SCALE) * norms, FLOOR)

    def chunk(first, count):
        for k in range(count):
            s, t = lists_smem[first + k], lists_smem[room + first + k]
            z = jnp.dot(x_ref[s], y_ref[t], preferred_element_type=jnp.float32) * SCALE + norm_ref[pl.ds(t, 1), :]
            z_ref[first + k] = z
            acc_ref[s] += jnp.exp2(z)
            touched_ref[pl.ds(t, 1), :] = jnp.ones((1, size), jnp.float32)

    whole = pairs // LARGE_CHUNK

    def large(c, carry):
        chunk(c * LARGE_CHUNK, LARGE_CHUNK)
        return carry

    def rest(c, carry):
        chunk(whole * LARGE_CHUNK + c * CHUNK, CHUNK)
        return carry

    lax.fori_loop(0, whole, large, 0)
    lax.fori_loop(0, (pairs - whole * LARGE_CHUNK + CHUNK - 1) // CHUNK, rest, 0)
    touched_ref[pl.ds(0, targets), :] = jnp.where(mask, touched_ref[pl.ds(0, targets), :], 0.0)
    collect(acc_ref, sum_ref)
    valid = live_ref[...] > 0.0
    row_result(sum_ref[...], 0.0, valid, z_ref, None, lists_smem, pairs, out_ref)
    copy_lists.wait()


def col_kernel(n_parts, has_q, last, lists_ref, z_ref, touched_ref, logw_ref, *rest):
    q_ref, rest = (rest[0], rest[1:]) if has_q else (None, rest)
    parts, rest = rest[:n_parts], rest[n_parts:]
    if last:
        field_any, out_ref, field_ref, p_ref, pb_ref, lists_smem, acc_ref, top_ref, sems = rest
    else:
        p_ref, out_ref, pb_ref, lists_smem, acc_ref, top_ref, sems = rest
    copy = pltpu.make_async_copy(lists_ref, lists_smem, sems.at[0])
    copy.start()
    valid, total = merged([part[...] for part in parts])
    p_ref[...] = jnp.where(valid, LOG2E * logw_ref[...] - total, 0.0)
    if last:
        field_ref[...] = p_ref[...] * FIELD
        copy_field = pltpu.make_async_copy(field_ref, field_any, sems.at[1])
        copy_field.start()
    spread(p_ref, pb_ref)
    copy.wait()
    room = lists_smem.shape[0] // 2
    col_pass(
        z_ref, pb_ref, q_ref, touched_ref, lists_smem, lists_smem[room - 1], acc_ref, top_ref, out_ref
    )
    if last:
        copy_field.wait()


def row_kernel(n_parts, lists_ref, z_ref, p_ref, pb_ref, earlier_ref, logw_ref, *rest):
    parts, (q_ref, out_ref, lists_smem, acc_ref, sum_ref, sem) = rest[:n_parts], rest[n_parts:]
    targets = logw_ref.shape[0]
    copy = pltpu.make_async_copy(lists_ref, lists_smem, sem)
    copy.start()
    valid, total = merged([part[...] for part in parts])
    q_ref[pl.ds(0, targets), :] = jnp.where(valid, LOG2E * logw_ref[...] - total, 0.0)
    q_ref[pl.ds(targets, 8), :] = jnp.zeros((8, q_ref.shape[1]), jnp.float32)
    acc_ref[...] = jnp.zeros_like(acc_ref)
    copy.wait()
    room = lists_smem.shape[0] // 2
    pairs = lists_smem[room - 1]

    def chunk(c, carry):
        for k in range(CHUNK):
            s, t = lists_smem[c * CHUNK + k], lists_smem[room + c * CHUNK + k]
            acc_ref[s] += jnp.exp2(z_ref[c * CHUNK + k] + pb_ref[s] + q_ref[pl.ds(t, 1), :])
        return carry

    lax.fori_loop(0, (pairs + CHUNK - 1) // CHUNK, chunk, 0)
    collect(acc_ref, sum_ref)
    row_result(
        sum_ref[...], p_ref[...], earlier_ref[...] > ABSENT, z_ref, q_ref,
        lists_smem, pairs, out_ref,
    )


def last_kernel(n_parts, logw_ref, *rest):
    parts, (out_ref,) = rest[:n_parts], rest[n_parts:]
    valid, total = merged([part[...] for part in parts])
    out_ref[...] = jnp.where(valid, (LOG2E * logw_ref[...] - total) * FIELD, 0.0)


def call(kernel, name, outs, scratch, args, spaces="v", spaces_out="v"):
    where = {"v": pltpu.VMEM, "h": pltpu.HBM}
    return pl.pallas_call(
        kernel,
        out_shape=outs,
        in_specs=[pl.BlockSpec(memory_space=where[k]) for k in (spaces * len(args))[: len(args)]],
        out_specs=[pl.BlockSpec(memory_space=where[k]) for k in (spaces_out * len(outs))[: len(outs)]],
        scratch_shapes=scratch,
        name=name,
        compiler_params=pltpu.CompilerParams(vmem_limit_bytes=VMEM_LIMIT),
    )(*args)


def in_hbm(array):
    return pltpu.with_memory_space_constraint(array, pltpu.HBM)


def exchanged(part, axis):
    size = lax.axis_size(axis)
    pieces = [part]
    for d in range(1, size):
        if size & (size - 1):
            pairs = [(i, (i + d) % size) for i in range(size)]
        else:
            pairs = [(i, i ^ d) for i in range(size)]
        pieces.append(lax.ppermute(part, axis, pairs))
    return pieces


def on_device(src_points, tgt_points, src_logw, tgt_logw, src_sizes, tgt_sizes, pattern, counts):
    blocks, size, dims = src_points.shape
    targets = tgt_points.shape[0]
    slots = pattern.shape[2]
    f32, i32, bf16 = jnp.float32, jnp.int32, jnp.bfloat16
    xt = jnp.swapaxes(src_points, 1, 2)
    yt = jnp.swapaxes(tgt_points, 1, 2)
    room = -(-(blocks * slots + CHUNK + 1) // 512) * 512
    struct = jax.ShapeDtypeStruct
    dma = pltpu.SemaphoreType.DMA
    wide = pltpu.VMEM((blocks, size, size), f32)
    sums = pltpu.VMEM((blocks, size), f32)
    acc_col = pltpu.VMEM(((targets + 8) * 8, size), f32)
    lists_smem = pltpu.SMEM((2 * room,), i32)

    z, touched, lists, row_part = call(
        first_kernel,
        "scores_and_rows",
        [
            struct((blocks * slots + CHUNK, size, size), f32),
            struct((targets + 8, size), f32),
            struct((2 * room,), i32),
            struct((blocks, size), f32),
        ],
        [
            pltpu.SMEM((blocks,), i32),
            pltpu.VMEM((1, targets), i32),
            pltpu.SMEM((slots, blocks), i32),
            pltpu.SMEM((blocks,), i32),
            lists_smem,
            pltpu.VMEM((blocks, dims, size), bf16),
            pltpu.VMEM((blocks, size, dims + EXTRA), bf16),
            pltpu.VMEM((targets + 1, dims + EXTRA, size), bf16),
            pltpu.VMEM((targets + 8, size), f32),
            pltpu.VMEM((targets * 8, size), f32),
            sums,
            wide,
            sums,
            dma((7,)),
        ],
        [in_hbm(array) for array in (src_sizes, tgt_sizes[None, :], pattern[:, 0, :].T, counts[:, 0], xt, yt)],
        "h",
    )
    first_part = row_part
    q = None
    for repeat in range(ITERS):
        last = repeat == ITERS - 1
        row_parts = exchanged(row_part, "col")
        results = call(
            functools.partial(col_kernel, len(row_parts), q is not None, last),
            "columns",
            [struct((blocks, size), f32), struct((targets, size), f32)]
            + ([] if last else [struct((blocks, size, size), f32)]),
            ([sums, sums, wide] if last else []) + [lists_smem, acc_col, acc_col, dma((2,))],
            [lists, z, touched, src_logw] + ([] if q is None else [q]) + row_parts,
            spaces_out="hv" if last else "vvv",
        )
        p, col_part, *pb = results
        col_parts = exchanged(col_part, "row")
        if not last:
            q, row_part = call(
                functools.partial(row_kernel, len(col_parts)),
                "rows",
                [struct((targets + 8, size), f32), struct((blocks, size), f32)],
                [lists_smem, wide, sums, dma],
                [lists, z, p, *pb, first_part, tgt_logw] + col_parts,
            )
    (field_g,) = call(
        functools.partial(last_kernel, len(col_parts)),
        "target_field",
        [struct((targets, size), f32)],
        [],
        [tgt_logw] + col_parts,
    )
    return p, field_g


def solution(mesh):
    return jax.shard_map(
        on_device,
        mesh=mesh,
        in_specs=(
            P(("groups", "row"), None, None),
            P(("groups", "col"), None, None),
            P(("groups", "row"), None),
            P(("groups", "col"), None),
            P(("groups", "row")),
            P(("groups", "col")),
            P(("groups", "row"), "col", None),
            P(("groups", "row"), "col"),
        ),
        out_specs=(P(("groups", "row"), None), P(("groups", "col"), None)),
        check_vma=False,
    )
```

```python
import functools
import math

import jax
import jax.numpy as jnp
from jax import lax
from jax.experimental import pallas as pl
from jax.experimental.pallas import tpu as pltpu
from jax.sharding import PartitionSpec as P

ITERS = 2
EPS = 0.5
LOG2E = math.log2(math.e)
SCALE = 2.0 / EPS * LOG2E
FIELD = EPS / LOG2E
FLOOR = -1e30
ABSENT = -1e29
SMALL = 2.0**-80
CHUNK = 16
LARGE_CHUNK = 128
EXTRA = 16
PIECES = 2
VMEM_LIMIT = 26 * 1024 * 1024


def eight(t):
    return pl.ds(pl.multiple_of(t * 8, 8), 8)


def folded(matrix):
    return matrix.reshape(-1, 8, matrix.shape[-1])


def every_eighth(ref, r, count):
    return ref[pl.ds(r, count, stride=8), :]


def merged(parts):
    top = functools.reduce(jnp.maximum, parts)
    total = top + jnp.log2(sum(jnp.exp2(part - top) for part in parts))
    return top > ABSENT, total


def spread(p_ref, pb_ref):
    blocks, size = p_ref.shape

    def body(s, carry):
        pb_ref[s] = jnp.broadcast_to(p_ref[pl.ds(s, 1), :], (size, size)).T
        return carry

    lax.fori_loop(0, blocks, body, 0, unroll=16)


def collect(acc_ref, sum_ref):
    def body(s, carry):
        sum_ref[pl.ds(s, 1), :] = jnp.sum(acc_ref[s].T, axis=0, keepdims=True)
        return carry

    lax.fori_loop(0, acc_ref.shape[0], body, 0, unroll=16)


def fetch(points):
    refs, sources, sems = points
    if sources is not None:
        copies = [pltpu.make_async_copy(source, ref, sems.at[k]) for k, (source, ref) in enumerate(zip(sources, refs))]
        for copy in copies:
            copy.start()
        for copy in copies:
            copy.wait()
    return refs


def score(scores, lists, p):
    x_ref, y_ref, norm_ref = scores
    s, t = lists[p], lists[lists.shape[0] // 2 + p]
    cross = jnp.dot(x_ref[s], y_ref[t], preferred_element_type=jnp.float32)
    return s, t, cross * SCALE + norm_ref[pl.ds(t, 1), :]


def row_result(total, shift, valid, points, q_ref, lists, pairs, out_ref):
    blocks, size = out_ref.shape
    out_ref[...] = jnp.where(valid, jnp.log2(jnp.maximum(total, SMALL)) + shift, FLOOR)
    lowest = jnp.min(jnp.where(valid, total, 1.0))

    @pl.when(lowest < SMALL)
    def _():
        scores = fetch(points)

        def term(p):
            _, t, z = score(scores, lists, p)
            return z if q_ref is None else z + q_ref[pl.ds(t, 1), :]

        def block(s, first):
            def same(p):
                return (p < pairs) & (lists[jnp.minimum(p, pairs - 1)] == s)

            def raise_top(carry):
                return carry[0] + 1, jnp.maximum(carry[1], term(carry[0]))

            start = (first, jnp.full((size, size), 16.0 * FLOOR, jnp.float32))
            end, top = lax.while_loop(lambda carry: same(carry[0]), raise_top, start)
            top = jnp.max(top, axis=1, keepdims=True)

            def add(p, acc):
                return acc + jnp.exp2(term(p) - top)

            acc = lax.fori_loop(first, end, add, jnp.zeros((size, size), jnp.float32))
            full = top + jnp.log2(jnp.sum(acc, axis=1, keepdims=True))
            out_ref[pl.ds(s, 1), :] = jnp.broadcast_to(full, (size, size)).T[:1, :]
            return end

        lax.fori_loop(0, blocks, block, 0)
        out_ref[...] = jnp.where(valid, out_ref[...], FLOOR)


def normalised(potential, valid):
    held = jnp.where(valid, potential, FLOOR)
    top = jnp.max(jnp.max(held, axis=0, keepdims=True), axis=1, keepdims=True)
    return top, jnp.exp2(held - top)


def col_pass(k_ref, mass_ref, top_p, points, p_ref, touched_ref, lists, pairs, acc_ref, top_ref, out_ref):
    targets, size = out_ref.shape
    room = lists.shape[0] // 2
    acc_ref[...] = jnp.zeros_like(acc_ref)

    def chunk(c, carry):
        for k in range(CHUNK):
            s, t = lists[c * CHUNK + k], lists[room + c * CHUNK + k]
            acc_ref[eight(t), :] += jnp.sum(folded(k_ref[c * CHUNK + k] * mass_ref[s]), axis=0)
        return carry

    lax.fori_loop(0, (pairs + CHUNK - 1) // CHUNK, chunk, 0)
    total = sum(every_eighth(acc_ref, r, targets) for r in range(8))
    valid = touched_ref[:targets, :] > 0.0
    out_ref[...] = jnp.where(valid, jnp.log2(jnp.maximum(total, SMALL)) + top_p, FLOOR)
    lowest = jnp.min(jnp.where(valid, total, 1.0))

    @pl.when(lowest < SMALL)
    def _():
        acc_ref[...] = jnp.zeros_like(acc_ref)
        top_ref[...] = jnp.full_like(top_ref, 16.0 * FLOOR)
        scores = fetch(points)

        def term(p):
            s, t, z = score(scores, lists, p)
            return t, z + jnp.broadcast_to(p_ref[pl.ds(s, 1), :], (size, size)).T

        def raise_top(p, carry):
            t, z = term(p)
            top_ref[eight(t), :] = jnp.maximum(top_ref[eight(t), :], jnp.max(folded(z), axis=0))
            return carry

        lax.fori_loop(0, pairs, raise_top, 0)
        top = functools.reduce(jnp.maximum, [every_eighth(top_ref, r, targets) for r in range(8)])
        out_ref[...] = top

        def add(p, carry):
            t, z = term(p)
            acc_ref[eight(t), :] += jnp.sum(folded(jnp.exp2(z - out_ref[pl.ds(t, 1), :])), axis=0)
            return carry

        lax.fori_loop(0, pairs, add, 0)
        exact = sum(every_eighth(acc_ref, r, targets) for r in range(8))
        out_ref[...] = jnp.where(valid, top + jnp.log2(jnp.maximum(exact, 1.0)), FLOOR)


def three_terms(row):
    high = row.astype(jnp.bfloat16)
    rest = row - high.astype(jnp.float32)
    middle = rest.astype(jnp.bfloat16)
    low = (rest - middle.astype(jnp.float32)).astype(jnp.bfloat16)
    return [high.astype(jnp.float32), middle.astype(jnp.float32), low.astype(jnp.float32)]


def extra_rows(row):
    place = lax.broadcasted_iota(jnp.int32, (EXTRA, row.shape[1]), 0)
    result = jnp.zeros(place.shape, jnp.float32)
    for k, term in enumerate(three_terms(row)):
        result = jnp.where(place == k, term, result)
    return result


def first_kernel(
    ssz_any, tsz_any, pat_any, cnt_any, xt_any, yt_any,
    k_ref, touched_ref, lists_ref, out_ref, x_any, y_any, norm_any,
    ssz_ref, tsz_ref, pat_ref, cnt_ref, lists_smem, xt_ref, x_ref, y_ref, norm_ref, part_ref, live_ref, acc_ref, sum_ref,
    sems, sems_out,
):
    blocks, size = out_ref.shape
    dims = xt_ref.shape[1]
    targets = yt_any.shape[0]
    slots = pat_ref.shape[0]
    room = lists_smem.shape[0] // 2
    small = [
        pltpu.make_async_copy(source, target, sems.at[k])
        for k, (source, target) in enumerate(
            [(ssz_any, ssz_ref), (tsz_any, tsz_ref), (pat_any, pat_ref), (cnt_any, cnt_ref)]
        )
    ]
    copy_x = pltpu.make_async_copy(xt_any, xt_ref, sems.at[4])
    piece = targets // PIECES
    copies_y = [
        pltpu.make_async_copy(
            yt_any.at[pl.ds(k * piece, piece)], y_ref.at[pl.ds(k * piece, piece), pl.ds(0, dims), :], sems.at[6 + k]
        )
        for k in range(PIECES)
    ]
    for copy in small:
        copy.start()
    copy_x.start()
    for copy in copies_y:
        copy.start()
    acc_ref[...] = jnp.zeros_like(acc_ref)
    touched_ref[...] = jnp.zeros_like(touched_ref)
    lanes = lax.broadcasted_iota(jnp.int32, (1, size), 1)
    ones = (lax.broadcasted_iota(jnp.int32, (EXTRA, size), 0) < 3).astype(jnp.bfloat16)

    def pad_rows(t, carry):
        y_ref[t, pl.ds(dims, EXTRA), :] = ones
        return carry

    lax.fori_loop(0, targets, pad_rows, 0, unroll=16)
    y_ref[targets] = jnp.zeros(y_ref.shape[1:], jnp.bfloat16)
    norm_ref[pl.ds(targets, 8), :] = jnp.full((8, size), FLOOR, jnp.float32)
    for copy in small:
        copy.wait()
    copy_x.wait()

    def source(s, p):
        xt = xt_ref[s].astype(jnp.float32)
        live = lanes < ssz_ref[s]
        norm = jnp.where(live, -0.5 * jnp.sum(xt * xt, axis=0, keepdims=True), FLOOR)
        live_ref[pl.ds(s, 1), :] = live.astype(jnp.float32)
        x_ref[s] = jnp.concatenate([xt, extra_rows(norm)], axis=0).T.astype(jnp.bfloat16)
        count = cnt_ref[s]
        for k in range(slots):
            lists_smem[p] = s
            lists_smem[room + p] = pat_ref[k, s]
            p = p + (k < count).astype(jnp.int32)
        return p

    pairs = lax.fori_loop(0, blocks, source, 0, unroll=8)
    for k in range(CHUNK):
        lists_smem[pairs + k] = blocks - 1
        lists_smem[room + pairs + k] = targets
    lists_smem[room - 1] = pairs
    copy_lists = pltpu.make_async_copy(lists_smem, lists_ref, sems.at[5])
    copy_lists.start()

    def target(t, carry):
        yt = y_ref[t, pl.ds(0, dims), :].astype(jnp.float32)
        part_ref[eight(t), :] = jnp.sum(folded(yt * yt), axis=0)
        return carry

    for k, copy in enumerate(copies_y):
        copy.wait()
        lax.fori_loop(k * piece, (k + 1) * piece, target, 0, unroll=16)
    sizes = jnp.broadcast_to(tsz_ref[...].astype(jnp.float32), (size, targets)).T
    mask = lax.broadcasted_iota(jnp.int32, (targets, size), 1).astype(jnp.float32) < sizes
    norms = sum(every_eighth(part_ref, r, targets) for r in range(8))
    norm_ref[pl.ds(0, targets), :] = jnp.where(mask, (-0.5 * SCALE) * norms, FLOOR)

    copies_out = [
        pltpu.make_async_copy(source, target, sems_out.at[k])
        for k, (source, target) in enumerate([(x_ref, x_any), (y_ref, y_any), (norm_ref, norm_any)])
    ]
    for copy in copies_out:
        copy.start()

    def chunk(first, count):
        for k in range(count):
            s, t = lists_smem[first + k], lists_smem[room + first + k]
            z = jnp.dot(x_ref[s], y_ref[t], preferred_element_type=jnp.float32) * SCALE + norm_ref[pl.ds(t, 1), :]
            mass = jnp.exp2(z)
            k_ref[first + k] = mass
            acc_ref[s] += mass
            touched_ref[pl.ds(t, 1), :] = jnp.ones((1, size), jnp.float32)

    whole = pairs // LARGE_CHUNK

    def large(c, carry):
        chunk(c * LARGE_CHUNK, LARGE_CHUNK)
        return carry

    def rest(c, carry):
        chunk(whole * LARGE_CHUNK + c * CHUNK, CHUNK)
        return carry

    lax.fori_loop(0, whole, large, 0)
    lax.fori_loop(0, (pairs - whole * LARGE_CHUNK + CHUNK - 1) // CHUNK, rest, 0)
    touched_ref[pl.ds(0, targets), :] = jnp.where(mask, touched_ref[pl.ds(0, targets), :], 0.0)
    collect(acc_ref, sum_ref)
    valid = live_ref[...] > 0.0
    points = ((x_ref, y_ref, norm_ref), None, None)
    row_result(sum_ref[...], 0.0, valid, points, None, lists_smem, pairs, out_ref)
    for copy in [copy_lists, *copies_out]:
        copy.wait()


def col_kernel(n_parts, last, lists_ref, k_ref, touched_ref, logw_ref, x_any, y_any, norm_any, *rest):
    parts, rest = rest[:n_parts], rest[n_parts:]
    if last:
        field_any, out_ref, field_ref, *rest = rest
    else:
        out_ref, *rest = rest
    p_ref, mass_ref, lists_smem, acc_ref, top_ref, x_ref, y_ref, norm_ref, sems = rest
    copy = pltpu.make_async_copy(lists_ref, lists_smem, sems.at[0])
    copy.start()
    valid, total = merged([part[...] for part in parts])
    p = jnp.where(valid, LOG2E * logw_ref[...] - total, 0.0)
    if last:
        field_ref[...] = p * FIELD
        copy_field = pltpu.make_async_copy(field_ref, field_any, sems.at[1])
        copy_field.start()
    top_p, mass = normalised(p, valid)
    p_ref[...] = mass
    spread(p_ref, mass_ref)
    p_ref[...] = p
    copy.wait()
    room = lists_smem.shape[0] // 2
    points = ((x_ref, y_ref, norm_ref), (x_any, y_any, norm_any), sems)
    col_pass(
        k_ref, mass_ref, top_p, points, p_ref, touched_ref, lists_smem, lists_smem[room - 1],
        acc_ref, top_ref, out_ref,
    )
    if last:
        copy_field.wait()


def row_kernel(n_parts, lists_ref, k_ref, earlier_ref, logw_ref, x_any, y_any, norm_any, *rest):
    parts, rest = rest[:n_parts], rest[n_parts:]
    out_ref, q_ref, mass_ref, lists_smem, acc_ref, sum_ref, x_ref, y_ref, norm_ref, sems = rest
    targets, size = logw_ref.shape
    copy = pltpu.make_async_copy(lists_ref, lists_smem, sems.at[0])
    copy.start()
    valid, total = merged([part[...] for part in parts])
    q = jnp.where(valid, LOG2E * logw_ref[...] - total, 0.0)
    q_ref[...] = q
    top_q, mass = normalised(q, valid)
    mass_ref[pl.ds(0, targets), :] = mass
    mass_ref[pl.ds(targets, 8), :] = jnp.zeros((8, size), jnp.float32)
    acc_ref[...] = jnp.zeros_like(acc_ref)
    copy.wait()
    room = lists_smem.shape[0] // 2
    pairs = lists_smem[room - 1]

    def chunk(c, carry):
        for k in range(CHUNK):
            s, t = lists_smem[c * CHUNK + k], lists_smem[room + c * CHUNK + k]
            acc_ref[s] += k_ref[c * CHUNK + k] * mass_ref[pl.ds(t, 1), :]
        return carry

    lax.fori_loop(0, (pairs + CHUNK - 1) // CHUNK, chunk, 0)
    collect(acc_ref, sum_ref)
    points = ((x_ref, y_ref, norm_ref), (x_any, y_any, norm_any), sems)
    row_result(sum_ref[...], top_q, earlier_ref[...] > ABSENT, points, q_ref, lists_smem, pairs, out_ref)


def last_kernel(n_parts, logw_ref, *rest):
    parts, (out_ref,) = rest[:n_parts], rest[n_parts:]
    valid, total = merged([part[...] for part in parts])
    out_ref[...] = jnp.where(valid, (LOG2E * logw_ref[...] - total) * FIELD, 0.0)


def call(kernel, name, outs, scratch, args, spaces="v", spaces_out="v"):
    where = {"v": pltpu.VMEM, "h": pltpu.HBM}
    return pl.pallas_call(
        kernel,
        out_shape=outs,
        in_specs=[pl.BlockSpec(memory_space=where[k]) for k in (spaces * len(args))[: len(args)]],
        out_specs=[pl.BlockSpec(memory_space=where[k]) for k in (spaces_out * len(outs))[: len(outs)]],
        scratch_shapes=scratch,
        name=name,
        compiler_params=pltpu.CompilerParams(vmem_limit_bytes=VMEM_LIMIT),
    )(*args)


def in_hbm(array):
    return pltpu.with_memory_space_constraint(array, pltpu.HBM)


def exchanged(part, axis):
    size = lax.axis_size(axis)
    pieces = [part]
    for d in range(1, size):
        if size & (size - 1):
            pairs = [(i, (i + d) % size) for i in range(size)]
        else:
            pairs = [(i, i ^ d) for i in range(size)]
        pieces.append(lax.ppermute(part, axis, pairs))
    return pieces


def on_device(src_points, tgt_points, src_logw, tgt_logw, src_sizes, tgt_sizes, pattern, counts):
    blocks, size, dims = src_points.shape
    targets = tgt_points.shape[0]
    slots = pattern.shape[2]
    f32, i32, bf16 = jnp.float32, jnp.int32, jnp.bfloat16
    xt = jnp.swapaxes(src_points, 1, 2)
    yt = jnp.swapaxes(tgt_points, 1, 2)
    room = -(-(blocks * slots + CHUNK + 1) // 512) * 512
    struct = jax.ShapeDtypeStruct
    dma = pltpu.SemaphoreType.DMA
    wide = pltpu.VMEM((blocks, size, size), f32)
    sums = pltpu.VMEM((blocks, size), f32)
    acc_col = pltpu.VMEM(((targets + 8) * 8, size), f32)
    lists_smem = pltpu.SMEM((2 * room,), i32)

    points_vmem = [
        pltpu.VMEM((blocks, size, dims + EXTRA), bf16),
        pltpu.VMEM((targets + 1, dims + EXTRA, size), bf16),
        pltpu.VMEM((targets + 8, size), f32),
    ]

    k, touched, lists, row_part, *points = call(
        first_kernel,
        "kernel_and_rows",
        [
            struct((blocks * slots + CHUNK, size, size), f32),
            struct((targets + 8, size), f32),
            struct((2 * room,), i32),
            struct((blocks, size), f32),
            pltpu.HBM((blocks, size, dims + EXTRA), bf16),
            pltpu.HBM((targets + 1, dims + EXTRA, size), bf16),
            pltpu.HBM((targets + 8, size), f32),
        ],
        [
            pltpu.SMEM((blocks,), i32),
            pltpu.VMEM((1, targets), i32),
            pltpu.SMEM((slots, blocks), i32),
            pltpu.SMEM((blocks,), i32),
            lists_smem,
            pltpu.VMEM((blocks, dims, size), bf16),
            *points_vmem,
            pltpu.VMEM((targets * 8, size), f32),
            sums,
            wide,
            sums,
            dma((6 + PIECES,)),
            dma((3,)),
        ],
        [
            in_hbm(array)
            for array in (src_sizes, tgt_sizes[None, :], pattern[:, 0, :].T, counts[:, 0], xt, yt)
        ],
        "h",
        "vvvvhhh",
    )
    first_part = row_part
    points = [in_hbm(array) for array in points]
    for repeat in range(ITERS):
        last = repeat == ITERS - 1
        row_parts = exchanged(row_part, "col")
        *field_f, col_part = call(
            functools.partial(col_kernel, len(row_parts), last),
            "columns",
            ([struct((blocks, size), f32)] if last else []) + [struct((targets, size), f32)],
            ([sums] if last else []) + [sums, wide, lists_smem, acc_col, acc_col, *points_vmem, dma((3,))],
            [lists, k, touched, src_logw, *points, *row_parts],
            "vvvvhhh" + "v" * len(row_parts),
            spaces_out="hv" if last else "v",
        )
        col_parts = exchanged(col_part, "row")
        if not last:
            (row_part,) = call(
                functools.partial(row_kernel, len(col_parts)),
                "rows",
                [struct((blocks, size), f32)],
                [
                    pltpu.VMEM((targets, size), f32),
                    pltpu.VMEM((targets + 8, size), f32),
                    lists_smem,
                    wide,
                    sums,
                    *points_vmem,
                    dma((3,)),
                ],
                [lists, k, first_part, tgt_logw, *points, *col_parts],
                "vvvvhhh" + "v" * len(col_parts),
            )
    (field_g,) = call(
        functools.partial(last_kernel, len(col_parts)),
        "target_field",
        [struct((targets, size), f32)],
        [],
        [tgt_logw] + col_parts,
    )
    return field_f[0], field_g


def solution(mesh):
    return jax.shard_map(
        on_device,
        mesh=mesh,
        in_specs=(
            P(("groups", "row"), None, None),
            P(("groups", "col"), None, None),
            P(("groups", "row"), None),
            P(("groups", "col"), None),
            P(("groups", "row")),
            P(("groups", "col")),
            P(("groups", "row"), "col", None),
            P(("groups", "row"), "col"),
        ),
        out_specs=(P(("groups", "row"), None), P(("groups", "col"), None)),
        check_vma=False,
    )
```

```python
import functools
import math

import jax
import jax.numpy as jnp
from jax import lax
from jax.experimental import pallas as pl
from jax.experimental.pallas import tpu as pltpu
from jax.sharding import PartitionSpec as P

ITERS = 2
EPS = 0.5
LOG2E = math.log2(math.e)
SCALE = 2.0 / EPS * LOG2E
FIELD = EPS / LOG2E
FLOOR = -1e30
ABSENT = -1e29
SMALL = 2.0**-80
CHUNK = 16
LARGE_CHUNK = 128
EXTRA = 16
PIECES = 2
VMEM_LIMIT = 26 * 1024 * 1024


def eight(t):
    return pl.ds(pl.multiple_of(t * 8, 8), 8)


def folded(matrix):
    return matrix.reshape(-1, 8, matrix.shape[-1])


def every_eighth(ref, r, count):
    return ref[pl.ds(r, count, stride=8), :]


def merged(parts):
    top = functools.reduce(jnp.maximum, parts)
    total = top + jnp.log2(sum(jnp.exp2(part - top) for part in parts))
    return top > ABSENT, total


def spread(p_ref, pb_ref):
    blocks, size = p_ref.shape

    def body(s, carry):
        pb_ref[s] = jnp.broadcast_to(p_ref[pl.ds(s, 1), :], (size, size)).T
        return carry

    lax.fori_loop(0, blocks, body, 0, unroll=16)


def collect(acc_ref, sum_ref):
    def body(s, carry):
        sum_ref[pl.ds(s, 1), :] = jnp.sum(acc_ref[s].T, axis=0, keepdims=True)
        return carry

    lax.fori_loop(0, acc_ref.shape[0], body, 0, unroll=16)


def fetch(points):
    refs, sources, sems = points
    if sources is not None:
        copies = [pltpu.make_async_copy(source, ref, sems.at[k]) for k, (source, ref) in enumerate(zip(sources, refs))]
        for copy in copies:
            copy.start()
        for copy in copies:
            copy.wait()
    return refs


def score(scores, lists, p):
    x_ref, y_ref, norm_ref = scores
    s, t = lists[p], lists[lists.shape[0] // 2 + p]
    cross = jnp.dot(x_ref[s], y_ref[t], preferred_element_type=jnp.float32)
    return s, t, cross * SCALE + norm_ref[pl.ds(t, 1), :]


def row_result(total, shift, valid, points, q_ref, lists, pairs, out_ref):
    blocks, size = out_ref.shape
    out_ref[...] = jnp.where(valid, jnp.log2(jnp.maximum(total, SMALL)) + shift, FLOOR)
    lowest = jnp.min(jnp.where(valid, total, 1.0))

    @pl.when(lowest < SMALL)
    def _():
        scores = fetch(points)

        def term(p):
            _, t, z = score(scores, lists, p)
            return z if q_ref is None else z + q_ref[pl.ds(t, 1), :]

        def block(s, first):
            def same(p):
                return (p < pairs) & (lists[jnp.minimum(p, pairs - 1)] == s)

            def raise_top(carry):
                return carry[0] + 1, jnp.maximum(carry[1], term(carry[0]))

            start = (first, jnp.full((size, size), 16.0 * FLOOR, jnp.float32))
            end, top = lax.while_loop(lambda carry: same(carry[0]), raise_top, start)
            top = jnp.max(top, axis=1, keepdims=True)

            def add(p, acc):
                return acc + jnp.exp2(term(p) - top)

            acc = lax.fori_loop(first, end, add, jnp.zeros((size, size), jnp.float32))
            full = top + jnp.log2(jnp.sum(acc, axis=1, keepdims=True))
            out_ref[pl.ds(s, 1), :] = jnp.broadcast_to(full, (size, size)).T[:1, :]
            return end

        lax.fori_loop(0, blocks, block, 0)
        out_ref[...] = jnp.where(valid, out_ref[...], FLOOR)


def normalised(potential, valid):
    held = jnp.where(valid, potential, FLOOR)
    top = jnp.max(jnp.max(held, axis=0, keepdims=True), axis=1, keepdims=True)
    return top, jnp.exp2(held - top)


def col_pass(k_ref, mass_ref, top_p, points, p_ref, touched_ref, lists, pairs, acc_ref, top_ref, out_ref):
    targets, size = out_ref.shape
    room = lists.shape[0] // 2
    acc_ref[...] = jnp.zeros_like(acc_ref)

    def chunk(c, carry):
        for k in range(CHUNK):
            s, t = lists[c * CHUNK + k], lists[room + c * CHUNK + k]
            acc_ref[eight(t), :] += jnp.sum(folded(k_ref[c * CHUNK + k] * mass_ref[s]), axis=0)
        return carry

    lax.fori_loop(0, (pairs + CHUNK - 1) // CHUNK, chunk, 0)
    total = sum(every_eighth(acc_ref, r, targets) for r in range(8))
    valid = touched_ref[:targets, :] > 0.0
    out_ref[...] = jnp.where(valid, jnp.log2(jnp.maximum(total, SMALL)) + top_p, FLOOR)
    lowest = jnp.min(jnp.where(valid, total, 1.0))

    @pl.when(lowest < SMALL)
    def _():
        acc_ref[...] = jnp.zeros_like(acc_ref)
        top_ref[...] = jnp.full_like(top_ref, 16.0 * FLOOR)
        scores = fetch(points)

        def term(p):
            s, t, z = score(scores, lists, p)
            return t, z + jnp.broadcast_to(p_ref[pl.ds(s, 1), :], (size, size)).T

        def raise_top(p, carry):
            t, z = term(p)
            top_ref[eight(t), :] = jnp.maximum(top_ref[eight(t), :], jnp.max(folded(z), axis=0))
            return carry

        lax.fori_loop(0, pairs, raise_top, 0)
        top = functools.reduce(jnp.maximum, [every_eighth(top_ref, r, targets) for r in range(8)])
        out_ref[...] = top

        def add(p, carry):
            t, z = term(p)
            acc_ref[eight(t), :] += jnp.sum(folded(jnp.exp2(z - out_ref[pl.ds(t, 1), :])), axis=0)
            return carry

        lax.fori_loop(0, pairs, add, 0)
        exact = sum(every_eighth(acc_ref, r, targets) for r in range(8))
        out_ref[...] = jnp.where(valid, top + jnp.log2(jnp.maximum(exact, 1.0)), FLOOR)


def three_terms(row):
    high = row.astype(jnp.bfloat16)
    rest = row - high.astype(jnp.float32)
    middle = rest.astype(jnp.bfloat16)
    low = (rest - middle.astype(jnp.float32)).astype(jnp.bfloat16)
    return [high.astype(jnp.float32), middle.astype(jnp.float32), low.astype(jnp.float32)]


def extra_rows(row):
    place = lax.broadcasted_iota(jnp.int32, (EXTRA, row.shape[1]), 0)
    result = jnp.zeros(place.shape, jnp.float32)
    for k, term in enumerate(three_terms(row)):
        result = jnp.where(place == k, term, result)
    return result


def first_kernel(
    ssz_any, tsz_any, pat_any, cnt_any, xt_any, yt_any,
    k_ref, touched_ref, lists_smem, out_ref, x_any, y_any, norm_any,
    ssz_ref, tsz_ref, pat_ref, cnt_ref, xt_ref, x_ref, y_ref, norm_ref, part_ref, live_ref, acc_ref, sum_ref,
    sems, sems_out,
):
    blocks, size = out_ref.shape
    dims = xt_ref.shape[1]
    targets = yt_any.shape[0]
    slots = pat_ref.shape[0]
    room = lists_smem.shape[0] // 2
    small = [
        pltpu.make_async_copy(source, target, sems.at[k])
        for k, (source, target) in enumerate(
            [(ssz_any, ssz_ref), (tsz_any, tsz_ref), (pat_any, pat_ref), (cnt_any, cnt_ref)]
        )
    ]
    copy_x = pltpu.make_async_copy(xt_any, xt_ref, sems.at[4])
    piece = targets // PIECES
    copies_y = [
        pltpu.make_async_copy(
            yt_any.at[pl.ds(k * piece, piece)], y_ref.at[pl.ds(k * piece, piece), pl.ds(0, dims), :], sems.at[6 + k]
        )
        for k in range(PIECES)
    ]
    for copy in small:
        copy.start()
    copy_x.start()
    for copy in copies_y:
        copy.start()
    acc_ref[...] = jnp.zeros_like(acc_ref)
    touched_ref[...] = jnp.zeros_like(touched_ref)
    lanes = lax.broadcasted_iota(jnp.int32, (1, size), 1)
    ones = (lax.broadcasted_iota(jnp.int32, (EXTRA, size), 0) < 3).astype(jnp.bfloat16)

    def pad_rows(t, carry):
        y_ref[t, pl.ds(dims, EXTRA), :] = ones
        return carry

    lax.fori_loop(0, targets, pad_rows, 0, unroll=16)
    y_ref[targets] = jnp.zeros(y_ref.shape[1:], jnp.bfloat16)
    norm_ref[pl.ds(targets, 8), :] = jnp.full((8, size), FLOOR, jnp.float32)
    for copy in small:
        copy.wait()
    copy_x.wait()

    def source(s, p):
        xt = xt_ref[s].astype(jnp.float32)
        live = lanes < ssz_ref[s]
        norm = jnp.where(live, -0.5 * jnp.sum(xt * xt, axis=0, keepdims=True), FLOOR)
        live_ref[pl.ds(s, 1), :] = live.astype(jnp.float32)
        x_ref[s] = jnp.concatenate([xt, extra_rows(norm)], axis=0).T.astype(jnp.bfloat16)
        count = cnt_ref[s]
        for k in range(slots):
            lists_smem[p] = s
            lists_smem[room + p] = pat_ref[k, s]
            p = p + (k < count).astype(jnp.int32)
        return p

    pairs = lax.fori_loop(0, blocks, source, 0, unroll=8)
    for k in range(CHUNK):
        lists_smem[pairs + k] = blocks - 1
        lists_smem[room + pairs + k] = targets
    lists_smem[room - 1] = pairs

    def target(t, carry):
        yt = y_ref[t, pl.ds(0, dims), :].astype(jnp.float32)
        part_ref[eight(t), :] = jnp.sum(folded(yt * yt), axis=0)
        return carry

    for k, copy in enumerate(copies_y):
        copy.wait()
        lax.fori_loop(k * piece, (k + 1) * piece, target, 0, unroll=16)
    sizes = jnp.broadcast_to(tsz_ref[...].astype(jnp.float32), (size, targets)).T
    mask = lax.broadcasted_iota(jnp.int32, (targets, size), 1).astype(jnp.float32) < sizes
    norms = sum(every_eighth(part_ref, r, targets) for r in range(8))
    norm_ref[pl.ds(0, targets), :] = jnp.where(mask, (-0.5 * SCALE) * norms, FLOOR)

    copies_out = [
        pltpu.make_async_copy(source, target, sems_out.at[k])
        for k, (source, target) in enumerate([(x_ref, x_any), (y_ref, y_any), (norm_ref, norm_any)])
    ]
    for copy in copies_out:
        copy.start()

    def chunk(first, count):
        for k in range(count):
            s, t = lists_smem[first + k], lists_smem[room + first + k]
            z = jnp.dot(x_ref[s], y_ref[t], preferred_element_type=jnp.float32) * SCALE + norm_ref[pl.ds(t, 1), :]
            mass = jnp.exp2(z)
            k_ref[first + k] = mass
            acc_ref[s] += mass
            touched_ref[pl.ds(t, 1), :] = jnp.ones((1, size), jnp.float32)

    whole = pairs // LARGE_CHUNK

    def large(c, carry):
        chunk(c * LARGE_CHUNK, LARGE_CHUNK)
        return carry

    def rest(c, carry):
        chunk(whole * LARGE_CHUNK + c * CHUNK, CHUNK)
        return carry

    lax.fori_loop(0, whole, large, 0)
    lax.fori_loop(0, (pairs - whole * LARGE_CHUNK + CHUNK - 1) // CHUNK, rest, 0)
    touched_ref[pl.ds(0, targets), :] = jnp.where(mask, touched_ref[pl.ds(0, targets), :], 0.0)
    collect(acc_ref, sum_ref)
    valid = live_ref[...] > 0.0
    points = ((x_ref, y_ref, norm_ref), None, None)
    row_result(sum_ref[...], 0.0, valid, points, None, lists_smem, pairs, out_ref)
    for copy in copies_out:
        copy.wait()


def col_kernel(n_parts, last, lists_smem, k_ref, touched_ref, logw_ref, x_any, y_any, norm_any, *rest):
    parts, rest = rest[:n_parts], rest[n_parts:]
    if last:
        field_any, out_ref, field_ref, *rest = rest
    else:
        out_ref, *rest = rest
    p_ref, mass_ref, acc_ref, top_ref, x_ref, y_ref, norm_ref, sems = rest
    valid, total = merged([part[...] for part in parts])
    p = jnp.where(valid, LOG2E * logw_ref[...] - total, 0.0)
    if last:
        field_ref[...] = p * FIELD
        copy_field = pltpu.make_async_copy(field_ref, field_any, sems.at[1])
        copy_field.start()
    top_p, mass = normalised(p, valid)
    p_ref[...] = mass
    spread(p_ref, mass_ref)
    p_ref[...] = p
    room = lists_smem.shape[0] // 2
    points = ((x_ref, y_ref, norm_ref), (x_any, y_any, norm_any), sems)
    col_pass(
        k_ref, mass_ref, top_p, points, p_ref, touched_ref, lists_smem, lists_smem[room - 1],
        acc_ref, top_ref, out_ref,
    )
    if last:
        copy_field.wait()


def row_kernel(n_parts, lists_smem, k_ref, earlier_ref, logw_ref, x_any, y_any, norm_any, *rest):
    parts, rest = rest[:n_parts], rest[n_parts:]
    out_ref, q_ref, mass_ref, acc_ref, sum_ref, x_ref, y_ref, norm_ref, sems = rest
    targets, size = logw_ref.shape
    valid, total = merged([part[...] for part in parts])
    q = jnp.where(valid, LOG2E * logw_ref[...] - total, 0.0)
    q_ref[...] = q
    top_q, mass = normalised(q, valid)
    mass_ref[pl.ds(0, targets), :] = mass
    mass_ref[pl.ds(targets, 8), :] = jnp.zeros((8, size), jnp.float32)
    acc_ref[...] = jnp.zeros_like(acc_ref)
    room = lists_smem.shape[0] // 2
    pairs = lists_smem[room - 1]

    def chunk(c, carry):
        for k in range(CHUNK):
            s, t = lists_smem[c * CHUNK + k], lists_smem[room + c * CHUNK + k]
            acc_ref[s] += k_ref[c * CHUNK + k] * mass_ref[pl.ds(t, 1), :]
        return carry

    lax.fori_loop(0, (pairs + CHUNK - 1) // CHUNK, chunk, 0)
    collect(acc_ref, sum_ref)
    points = ((x_ref, y_ref, norm_ref), (x_any, y_any, norm_any), sems)
    row_result(sum_ref[...], top_q, earlier_ref[...] > ABSENT, points, q_ref, lists_smem, pairs, out_ref)


def last_kernel(n_parts, logw_ref, *rest):
    parts, (out_ref,) = rest[:n_parts], rest[n_parts:]
    valid, total = merged([part[...] for part in parts])
    out_ref[...] = jnp.where(valid, (LOG2E * logw_ref[...] - total) * FIELD, 0.0)


def call(kernel, name, outs, scratch, args, spaces="v", spaces_out="v"):
    where = {"v": pltpu.VMEM, "h": pltpu.HBM, "s": pltpu.SMEM}
    return pl.pallas_call(
        kernel,
        out_shape=outs,
        in_specs=[pl.BlockSpec(memory_space=where[k]) for k in (spaces * len(args))[: len(args)]],
        out_specs=[pl.BlockSpec(memory_space=where[k]) for k in (spaces_out * len(outs))[: len(outs)]],
        scratch_shapes=scratch,
        name=name,
        compiler_params=pltpu.CompilerParams(vmem_limit_bytes=VMEM_LIMIT),
    )(*args)


def in_hbm(array):
    return pltpu.with_memory_space_constraint(array, pltpu.HBM)


def exchanged(part, axis):
    size = lax.axis_size(axis)
    pieces = [part]
    for d in range(1, size):
        if size & (size - 1):
            pairs = [(i, (i + d) % size) for i in range(size)]
        else:
            pairs = [(i, i ^ d) for i in range(size)]
        pieces.append(lax.ppermute(part, axis, pairs))
    return pieces


def on_device(src_points, tgt_points, src_logw, tgt_logw, src_sizes, tgt_sizes, pattern, counts):
    blocks, size, dims = src_points.shape
    targets = tgt_points.shape[0]
    slots = pattern.shape[2]
    f32, i32, bf16 = jnp.float32, jnp.int32, jnp.bfloat16
    xt = jnp.swapaxes(src_points, 1, 2)
    yt = jnp.swapaxes(tgt_points, 1, 2)
    room = -(-(blocks * slots + CHUNK + 1) // 512) * 512
    struct = jax.ShapeDtypeStruct
    dma = pltpu.SemaphoreType.DMA
    wide = pltpu.VMEM((blocks, size, size), f32)
    sums = pltpu.VMEM((blocks, size), f32)
    acc_col = pltpu.VMEM(((targets + 8) * 8, size), f32)
    lists_smem = pltpu.SMEM((2 * room,), i32)

    points_vmem = [
        pltpu.VMEM((blocks, size, dims + EXTRA), bf16),
        pltpu.VMEM((targets + 1, dims + EXTRA, size), bf16),
        pltpu.VMEM((targets + 8, size), f32),
    ]

    k, touched, lists, row_part, *points = call(
        first_kernel,
        "kernel_and_rows",
        [
            struct((blocks * slots + CHUNK, size, size), f32),
            struct((targets + 8, size), f32),
            pltpu.SMEM((2 * room,), i32),
            struct((blocks, size), f32),
            pltpu.HBM((blocks, size, dims + EXTRA), bf16),
            pltpu.HBM((targets + 1, dims + EXTRA, size), bf16),
            pltpu.HBM((targets + 8, size), f32),
        ],
        [
            pltpu.SMEM((blocks,), i32),
            pltpu.VMEM((1, targets), i32),
            pltpu.SMEM((slots, blocks), i32),
            pltpu.SMEM((blocks,), i32),
            pltpu.VMEM((blocks, dims, size), bf16),
            *points_vmem,
            pltpu.VMEM((targets * 8, size), f32),
            sums,
            wide,
            sums,
            dma((6 + PIECES,)),
            dma((3,)),
        ],
        [
            in_hbm(array)
            for array in (src_sizes, tgt_sizes[None, :], pattern[:, 0, :].T, counts[:, 0], xt, yt)
        ],
        "h",
        "vvsvhhh",
    )
    first_part = row_part
    points = [in_hbm(array) for array in points]
    for repeat in range(ITERS):
        last = repeat == ITERS - 1
        row_parts = exchanged(row_part, "col")
        *field_f, col_part = call(
            functools.partial(col_kernel, len(row_parts), last),
            "columns",
            ([struct((blocks, size), f32)] if last else []) + [struct((targets, size), f32)],
            ([sums] if last else []) + [sums, wide, acc_col, acc_col, *points_vmem, dma((3,))],
            [lists, k, touched, src_logw, *points, *row_parts],
            "svvvhhh" + "v" * len(row_parts),
            spaces_out="hv" if last else "v",
        )
        col_parts = exchanged(col_part, "row")
        if not last:
            (row_part,) = call(
                functools.partial(row_kernel, len(col_parts)),
                "rows",
                [struct((blocks, size), f32)],
                [
                    pltpu.VMEM((targets, size), f32),
                    pltpu.VMEM((targets + 8, size), f32),
                    wide,
                    sums,
                    *points_vmem,
                    dma((3,)),
                ],
                [lists, k, first_part, tgt_logw, *points, *col_parts],
                "svvvhhh" + "v" * len(col_parts),
            )
    (field_g,) = call(
        functools.partial(last_kernel, len(col_parts)),
        "target_field",
        [struct((targets, size), f32)],
        [],
        [tgt_logw] + col_parts,
    )
    return field_f[0], field_g


def solution(mesh):
    return jax.shard_map(
        on_device,
        mesh=mesh,
        in_specs=(
            P(("groups", "row"), None, None),
            P(("groups", "col"), None, None),
            P(("groups", "row"), None),
            P(("groups", "col"), None),
            P(("groups", "row")),
            P(("groups", "col")),
            P(("groups", "row"), "col", None),
            P(("groups", "row"), "col"),
        ),
        out_specs=(P(("groups", "row"), None), P(("groups", "col"), None)),
        check_vma=False,
    )
```

```python
import functools
import math

import jax
import jax.numpy as jnp
from jax import lax
from jax.experimental import pallas as pl
from jax.experimental.pallas import tpu as pltpu
from jax.sharding import PartitionSpec as P

ITERS = 2
EPS = 0.5
LOG2E = math.log2(math.e)
SCALE = 2.0 / EPS * LOG2E
FIELD = EPS / LOG2E
FLOOR = -1e30
ABSENT = -1e29
SMALL = 2.0**-80
CHUNK = 32
LARGE_CHUNK = 128
EXTRA = 16
VMEM_LIMIT = 26 * 1024 * 1024


def eight(t):
    return pl.ds(pl.multiple_of(t * 8, 8), 8)


def folded(matrix):
    return matrix.reshape(-1, 8, matrix.shape[-1])


def halved(stack):
    while stack.shape[0] > 1:
        middle = stack.shape[0] // 2
        stack = stack[:middle] + stack[middle:]
    return stack[0]


def every_eighth(ref, r, count):
    return ref[pl.ds(r, count, stride=8), :]


def merged(parts):
    top = functools.reduce(jnp.maximum, parts)
    total = top + jnp.log2(sum(jnp.exp2(part - top) for part in parts))
    return top > ABSENT, total


def spread(p_ref, pb_ref):
    blocks, size = p_ref.shape

    def body(s, carry):
        pb_ref[s] = jnp.broadcast_to(p_ref[pl.ds(s, 1), :], (size, size)).T
        return carry

    lax.fori_loop(0, blocks, body, 0, unroll=32)


def collect(acc_ref, sum_ref):
    def body(s, carry):
        sum_ref[pl.ds(s, 1), :] = jnp.sum(acc_ref[s].T, axis=0, keepdims=True)
        return carry

    lax.fori_loop(0, acc_ref.shape[0], body, 0, unroll=32)


def fetch(points):
    refs, sources, sems = points
    if sources is not None:
        copies = [pltpu.make_async_copy(source, ref, sems.at[k]) for k, (source, ref) in enumerate(zip(sources, refs))]
        for copy in copies:
            copy.start()
        for copy in copies:
            copy.wait()
    return refs


def score(scores, lists, p):
    x_ref, y_ref, norm_ref = scores
    s, t = lists[p], lists[lists.shape[0] // 2 + p]
    cross = jnp.dot(x_ref[s], y_ref[t], preferred_element_type=jnp.float32)
    return s, t, cross * SCALE + norm_ref[pl.ds(t, 1), :]


def row_result(total, shift, valid, points, q_ref, lists, pairs, out_ref):
    blocks, size = out_ref.shape
    out_ref[...] = jnp.where(valid, jnp.log2(jnp.maximum(total, SMALL)) + shift, FLOOR)
    lowest = jnp.min(jnp.where(valid, total, 1.0))

    @pl.when(lowest < SMALL)
    def _():
        scores = fetch(points)

        def term(p):
            _, t, z = score(scores, lists, p)
            return z if q_ref is None else z + q_ref[pl.ds(t, 1), :]

        def block(s, first):
            def same(p):
                return (p < pairs) & (lists[jnp.minimum(p, pairs - 1)] == s)

            def raise_top(carry):
                return carry[0] + 1, jnp.maximum(carry[1], term(carry[0]))

            start = (first, jnp.full((size, size), 16.0 * FLOOR, jnp.float32))
            end, top = lax.while_loop(lambda carry: same(carry[0]), raise_top, start)
            top = jnp.max(top, axis=1, keepdims=True)

            def add(p, acc):
                return acc + jnp.exp2(term(p) - top)

            acc = lax.fori_loop(first, end, add, jnp.zeros((size, size), jnp.float32))
            full = top + jnp.log2(jnp.sum(acc, axis=1, keepdims=True))
            out_ref[pl.ds(s, 1), :] = jnp.broadcast_to(full, (size, size)).T[:1, :]
            return end

        lax.fori_loop(0, blocks, block, 0)
        out_ref[...] = jnp.where(valid, out_ref[...], FLOOR)


def normalised(potential, valid):
    held = jnp.where(valid, potential, FLOOR)
    top = jnp.max(jnp.max(held, axis=0, keepdims=True), axis=1, keepdims=True)
    return top, jnp.exp2(held - top)


def col_pass(k_ref, mass_ref, top_p, points, p_ref, touched_ref, lists, pairs, acc_ref, top_ref, out_ref):
    targets, size = out_ref.shape
    room = lists.shape[0] // 2
    acc_ref[...] = jnp.zeros_like(acc_ref)

    def chunk(c, carry):
        for k in range(CHUNK):
            s, t = lists[c * CHUNK + k], lists[room + c * CHUNK + k]
            acc_ref[eight(t), :] += halved(folded(k_ref[c * CHUNK + k] * mass_ref[s]))
        return carry

    lax.fori_loop(0, (pairs + CHUNK - 1) // CHUNK, chunk, 0)
    total = sum(every_eighth(acc_ref, r, targets) for r in range(8))
    valid = touched_ref[:targets, :] > 0.0
    out_ref[...] = jnp.where(valid, jnp.log2(jnp.maximum(total, SMALL)) + top_p, FLOOR)
    lowest = jnp.min(jnp.where(valid, total, 1.0))

    @pl.when(lowest < SMALL)
    def _():
        acc_ref[...] = jnp.zeros_like(acc_ref)
        top_ref[...] = jnp.full_like(top_ref, 16.0 * FLOOR)
        scores = fetch(points)

        def term(p):
            s, t, z = score(scores, lists, p)
            return t, z + jnp.broadcast_to(p_ref[pl.ds(s, 1), :], (size, size)).T

        def raise_top(p, carry):
            t, z = term(p)
            top_ref[eight(t), :] = jnp.maximum(top_ref[eight(t), :], jnp.max(folded(z), axis=0))
            return carry

        lax.fori_loop(0, pairs, raise_top, 0)
        top = functools.reduce(jnp.maximum, [every_eighth(top_ref, r, targets) for r in range(8)])
        out_ref[...] = top

        def add(p, carry):
            t, z = term(p)
            acc_ref[eight(t), :] += jnp.sum(folded(jnp.exp2(z - out_ref[pl.ds(t, 1), :])), axis=0)
            return carry

        lax.fori_loop(0, pairs, add, 0)
        exact = sum(every_eighth(acc_ref, r, targets) for r in range(8))
        out_ref[...] = jnp.where(valid, top + jnp.log2(jnp.maximum(exact, 1.0)), FLOOR)


def three_terms(row):
    high = row.astype(jnp.bfloat16)
    rest = row - high.astype(jnp.float32)
    middle = rest.astype(jnp.bfloat16)
    low = (rest - middle.astype(jnp.float32)).astype(jnp.bfloat16)
    return [high.astype(jnp.float32), middle.astype(jnp.float32), low.astype(jnp.float32)]


def extra_rows(row):
    place = lax.broadcasted_iota(jnp.int32, (EXTRA, row.shape[1]), 0)
    result = jnp.zeros(place.shape, jnp.float32)
    for k, term in enumerate(three_terms(row)):
        result = jnp.where(place == k, term, result)
    return result


def first_kernel(
    ssz_any, tsz_any, pat_any, cnt_any, xt_any, yt_any,
    k_ref, touched_ref, lists_smem, out_ref, x_any, y_any, norm_any,
    ssz_ref, tsz_ref, pat_ref, cnt_ref, xt_ref, x_ref, y_ref, norm_ref, part_ref, live_ref, acc_ref, sum_ref,
    sems, sems_out,
):
    blocks, size = out_ref.shape
    dims = xt_ref.shape[1]
    targets = yt_any.shape[0]
    slots = pat_ref.shape[0]
    room = lists_smem.shape[0] // 2
    small = [
        pltpu.make_async_copy(source, target, sems.at[k])
        for k, (source, target) in enumerate(
            [(ssz_any, ssz_ref), (tsz_any, tsz_ref), (pat_any, pat_ref), (cnt_any, cnt_ref)]
        )
    ]
    copy_x = pltpu.make_async_copy(xt_any, xt_ref, sems.at[4])
    copy_y = pltpu.make_async_copy(yt_any, y_ref.at[pl.ds(0, targets), pl.ds(0, dims), :], sems.at[5])
    for copy in small:
        copy.start()
    copy_x.start()
    copy_y.start()
    acc_ref[...] = jnp.zeros_like(acc_ref)
    touched_ref[...] = jnp.zeros_like(touched_ref)
    lanes = lax.broadcasted_iota(jnp.int32, (1, size), 1)
    ones = (lax.broadcasted_iota(jnp.int32, (EXTRA, size), 0) < 3).astype(jnp.bfloat16)

    def pad_rows(t, carry):
        y_ref[t, pl.ds(dims, EXTRA), :] = ones
        return carry

    lax.fori_loop(0, targets, pad_rows, 0, unroll=16)
    y_ref[targets] = jnp.zeros(y_ref.shape[1:], jnp.bfloat16)
    norm_ref[pl.ds(targets, 8), :] = jnp.full((8, size), FLOOR, jnp.float32)
    for copy in small:
        copy.wait()
    copy_x.wait()

    def source(s):
        xt = xt_ref[s].astype(jnp.float32)
        live = lanes < ssz_ref[s]
        norm = jnp.where(live, -0.5 * jnp.sum(xt * xt, axis=0, keepdims=True), FLOOR)
        live_ref[pl.ds(s, 1), :] = live.astype(jnp.float32)
        x_ref[s] = jnp.concatenate([xt, extra_rows(norm)], axis=0).T.astype(jnp.bfloat16)

    def target(t):
        yt = y_ref[t, pl.ds(0, dims), :].astype(jnp.float32)
        part_ref[eight(t), :] = jnp.sum(folded(yt * yt), axis=0)

    def list_block(s, p):
        count = cnt_ref[s]
        for k in range(slots):
            lists_smem[p] = s
            lists_smem[room + p] = pat_ref[k, s]
            p = p + (k < count).astype(jnp.int32)
        return p

    half = blocks // 2

    def with_sources(s, p):
        source(2 * s)
        source(2 * s + 1)
        return list_block(s, p)

    def with_targets(s, p):
        for k in range(targets // half):
            target(s * (targets // half) + k)
        return list_block(half + s, p)

    pairs = lax.fori_loop(0, half, with_sources, 0, unroll=16)
    copy_y.wait()
    pairs = lax.fori_loop(0, half, with_targets, pairs, unroll=16)
    for k in range(CHUNK):
        lists_smem[pairs + k] = blocks - 1
        lists_smem[room + pairs + k] = targets
    lists_smem[room - 1] = pairs
    sizes = jnp.broadcast_to(tsz_ref[...].astype(jnp.float32), (size, targets)).T
    mask = lax.broadcasted_iota(jnp.int32, (targets, size), 1).astype(jnp.float32) < sizes
    norms = sum(every_eighth(part_ref, r, targets) for r in range(8))
    norm_ref[pl.ds(0, targets), :] = jnp.where(mask, (-0.5 * SCALE) * norms, FLOOR)

    copies_out = [
        pltpu.make_async_copy(source, target, sems_out.at[k])
        for k, (source, target) in enumerate([(x_ref, x_any), (y_ref, y_any), (norm_ref, norm_any)])
    ]
    for copy in copies_out:
        copy.start()

    def chunk(first, count):
        for k in range(count):
            s, t = lists_smem[first + k], lists_smem[room + first + k]
            z = jnp.dot(x_ref[s], y_ref[t], preferred_element_type=jnp.float32) * SCALE + norm_ref[pl.ds(t, 1), :]
            mass = jnp.exp2(z)
            k_ref[first + k] = mass
            acc_ref[s] += mass
            touched_ref[pl.ds(t, 1), :] = jnp.ones((1, size), jnp.float32)

    whole = pairs // LARGE_CHUNK

    def large(c, carry):
        chunk(c * LARGE_CHUNK, LARGE_CHUNK)
        return carry

    def rest(c, carry):
        chunk(whole * LARGE_CHUNK + c * CHUNK, CHUNK)
        return carry

    lax.fori_loop(0, whole, large, 0)
    lax.fori_loop(0, (pairs - whole * LARGE_CHUNK + CHUNK - 1) // CHUNK, rest, 0)
    touched_ref[pl.ds(0, targets), :] = jnp.where(mask, touched_ref[pl.ds(0, targets), :], 0.0)
    collect(acc_ref, sum_ref)
    valid = live_ref[...] > 0.0
    points = ((x_ref, y_ref, norm_ref), None, None)
    row_result(sum_ref[...], 0.0, valid, points, None, lists_smem, pairs, out_ref)
    for copy in copies_out:
        copy.wait()


def col_kernel(n_parts, last, lists_smem, k_ref, touched_ref, logw_ref, x_any, y_any, norm_any, *rest):
    parts, rest = rest[:n_parts], rest[n_parts:]
    if last:
        field_any, out_ref, field_ref, *rest = rest
    else:
        out_ref, *rest = rest
    p_ref, mass_ref, acc_ref, top_ref, x_ref, y_ref, norm_ref, sems = rest
    valid, total = merged([part[...] for part in parts])
    p = jnp.where(valid, LOG2E * logw_ref[...] - total, 0.0)
    if last:
        field_ref[...] = p * FIELD
        copy_field = pltpu.make_async_copy(field_ref, field_any, sems.at[1])
        copy_field.start()
    top_p, mass = normalised(p, valid)
    p_ref[...] = mass
    spread(p_ref, mass_ref)
    p_ref[...] = p
    room = lists_smem.shape[0] // 2
    points = ((x_ref, y_ref, norm_ref), (x_any, y_any, norm_any), sems)
    col_pass(
        k_ref, mass_ref, top_p, points, p_ref, touched_ref, lists_smem, lists_smem[room - 1],
        acc_ref, top_ref, out_ref,
    )
    if last:
        copy_field.wait()


def row_kernel(n_parts, lists_smem, k_ref, earlier_ref, logw_ref, x_any, y_any, norm_any, *rest):
    parts, rest = rest[:n_parts], rest[n_parts:]
    out_ref, q_ref, mass_ref, acc_ref, sum_ref, x_ref, y_ref, norm_ref, sems = rest
    targets, size = logw_ref.shape
    valid, total = merged([part[...] for part in parts])
    q = jnp.where(valid, LOG2E * logw_ref[...] - total, 0.0)
    q_ref[...] = q
    top_q, mass = normalised(q, valid)
    mass_ref[pl.ds(0, targets), :] = mass
    mass_ref[pl.ds(targets, 8), :] = jnp.zeros((8, size), jnp.float32)
    acc_ref[...] = jnp.zeros_like(acc_ref)
    room = lists_smem.shape[0] // 2
    pairs = lists_smem[room - 1]

    def chunk(c, carry):
        for k in range(CHUNK):
            s, t = lists_smem[c * CHUNK + k], lists_smem[room + c * CHUNK + k]
            acc_ref[s] += k_ref[c * CHUNK + k] * mass_ref[pl.ds(t, 1), :]
        return carry

    lax.fori_loop(0, (pairs + CHUNK - 1) // CHUNK, chunk, 0)
    collect(acc_ref, sum_ref)
    points = ((x_ref, y_ref, norm_ref), (x_any, y_any, norm_any), sems)
    row_result(sum_ref[...], top_q, earlier_ref[...] > ABSENT, points, q_ref, lists_smem, pairs, out_ref)


def last_kernel(n_parts, logw_ref, *rest):
    parts, (out_ref,) = rest[:n_parts], rest[n_parts:]
    valid, total = merged([part[...] for part in parts])
    out_ref[...] = jnp.where(valid, (LOG2E * logw_ref[...] - total) * FIELD, 0.0)


def call(kernel, name, outs, scratch, args, spaces="v", spaces_out="v"):
    where = {"v": pltpu.VMEM, "h": pltpu.HBM, "s": pltpu.SMEM}
    return pl.pallas_call(
        kernel,
        out_shape=outs,
        in_specs=[pl.BlockSpec(memory_space=where[k]) for k in (spaces * len(args))[: len(args)]],
        out_specs=[pl.BlockSpec(memory_space=where[k]) for k in (spaces_out * len(outs))[: len(outs)]],
        scratch_shapes=scratch,
        name=name,
        compiler_params=pltpu.CompilerParams(vmem_limit_bytes=VMEM_LIMIT),
    )(*args)


def in_hbm(array):
    return pltpu.with_memory_space_constraint(array, pltpu.HBM)


def exchanged(part, axis):
    size = lax.axis_size(axis)
    pieces = [part]
    for d in range(1, size):
        if size & (size - 1):
            pairs = [(i, (i + d) % size) for i in range(size)]
        else:
            pairs = [(i, i ^ d) for i in range(size)]
        pieces.append(lax.ppermute(part, axis, pairs))
    return pieces


def on_device(src_points, tgt_points, src_logw, tgt_logw, src_sizes, tgt_sizes, pattern, counts):
    blocks, size, dims = src_points.shape
    targets = tgt_points.shape[0]
    slots = pattern.shape[2]
    f32, i32, bf16 = jnp.float32, jnp.int32, jnp.bfloat16
    xt = jnp.swapaxes(src_points, 1, 2)
    yt = jnp.swapaxes(tgt_points, 1, 2)
    room = -(-(blocks * slots + CHUNK + 1) // 512) * 512
    struct = jax.ShapeDtypeStruct
    dma = pltpu.SemaphoreType.DMA
    wide = pltpu.VMEM((blocks, size, size), f32)
    sums = pltpu.VMEM((blocks, size), f32)
    acc_col = pltpu.VMEM(((targets + 8) * 8, size), f32)
    lists_smem = pltpu.SMEM((2 * room,), i32)

    points_vmem = [
        pltpu.VMEM((blocks, size, dims + EXTRA), bf16),
        pltpu.VMEM((targets + 1, dims + EXTRA, size), bf16),
        pltpu.VMEM((targets + 8, size), f32),
    ]

    k, touched, lists, row_part, *points = call(
        first_kernel,
        "kernel_and_rows",
        [
            struct((blocks * slots + CHUNK, size, size), f32),
            struct((targets + 8, size), f32),
            pltpu.SMEM((2 * room,), i32),
            struct((blocks, size), f32),
            pltpu.HBM((blocks, size, dims + EXTRA), bf16),
            pltpu.HBM((targets + 1, dims + EXTRA, size), bf16),
            pltpu.HBM((targets + 8, size), f32),
        ],
        [
            pltpu.SMEM((blocks,), i32),
            pltpu.VMEM((1, targets), i32),
            pltpu.SMEM((slots, blocks), i32),
            pltpu.SMEM((blocks,), i32),
            pltpu.VMEM((blocks, dims, size), bf16),
            *points_vmem,
            pltpu.VMEM((targets * 8, size), f32),
            sums,
            wide,
            sums,
            dma((6,)),
            dma((3,)),
        ],
        [
            in_hbm(array)
            for array in (src_sizes, tgt_sizes[None, :], pattern[:, 0, :].T, counts[:, 0], xt, yt)
        ],
        "h",
        "vvsvhhh",
    )
    first_part = row_part
    points = [in_hbm(array) for array in points]
    for repeat in range(ITERS):
        last = repeat == ITERS - 1
        row_parts = exchanged(row_part, "col")
        *field_f, col_part = call(
            functools.partial(col_kernel, len(row_parts), last),
            "columns",
            ([struct((blocks, size), f32)] if last else []) + [struct((targets, size), f32)],
            ([sums] if last else []) + [sums, wide, acc_col, acc_col, *points_vmem, dma((3,))],
            [lists, k, touched, src_logw, *points, *row_parts],
            "svvvhhh" + "v" * len(row_parts),
            spaces_out="hv" if last else "v",
        )
        col_parts = exchanged(col_part, "row")
        if not last:
            (row_part,) = call(
                functools.partial(row_kernel, len(col_parts)),
                "rows",
                [struct((blocks, size), f32)],
                [
                    pltpu.VMEM((targets, size), f32),
                    pltpu.VMEM((targets + 8, size), f32),
                    wide,
                    sums,
                    *points_vmem,
                    dma((3,)),
                ],
                [lists, k, first_part, tgt_logw, *points, *col_parts],
                "svvvhhh" + "v" * len(col_parts),
            )
    (field_g,) = call(
        functools.partial(last_kernel, len(col_parts)),
        "target_field",
        [struct((targets, size), f32)],
        [],
        [tgt_logw] + col_parts,
    )
    return field_f[0], field_g


def solution(mesh):
    return jax.shard_map(
        on_device,
        mesh=mesh,
        in_specs=(
            P(("groups", "row"), None, None),
            P(("groups", "col"), None, None),
            P(("groups", "row"), None),
            P(("groups", "col"), None),
            P(("groups", "row")),
            P(("groups", "col")),
            P(("groups", "row"), "col", None),
            P(("groups", "row"), "col"),
        ),
        out_specs=(P(("groups", "row"), None), P(("groups", "col"), None)),
        check_vma=False,
    )
```

```python
import functools
import math

import jax
import jax.numpy as jnp
from jax import lax
from jax.experimental import pallas as pl
from jax.experimental.pallas import tpu as pltpu
from jax.sharding import PartitionSpec as P

ITERS = 2
EPS = 0.5
LOG2E = math.log2(math.e)
SCALE = 2.0 / EPS * LOG2E
FIELD = EPS / LOG2E
FLOOR = -1e30
ABSENT = -1e29
SMALL = 2.0**-80
CHUNK = 32
LARGE_CHUNK = 128
EXTRA = 16
VMEM_LIMIT = 26 * 1024 * 1024


def eight(t):
    return pl.ds(pl.multiple_of(t * 8, 8), 8)


def folded(matrix):
    return matrix.reshape(-1, 8, matrix.shape[-1])


def halved(stack):
    while stack.shape[0] > 1:
        middle = stack.shape[0] // 2
        stack = stack[:middle] + stack[middle:]
    return stack[0]


def every_eighth(ref, r, count):
    return ref[pl.ds(r, count, stride=8), :]


def merged(parts):
    top = functools.reduce(jnp.maximum, parts)
    total = top + jnp.log2(sum(jnp.exp2(part - top) for part in parts))
    return top > ABSENT, total


def spread(mass, pb_ref):
    blocks, size = mass.shape
    columns = jnp.concatenate([mass, jnp.zeros((size - blocks, size), jnp.float32)], axis=0).T
    terms = [term.astype(jnp.bfloat16) for term in three_terms(columns)]
    stacked = jnp.concatenate([term[:, :blocks] for term in terms] + [terms[2][:, blocks : size - 2 * blocks]], axis=1)
    block = lax.broadcasted_iota(jnp.int32, (size, size), 0) % blocks
    for s in range(blocks):
        if s % 2:
            chosen = jnp.where(block == s, 1.0, 0.0).astype(jnp.bfloat16)
            pb_ref[s] = jnp.dot(stacked, chosen, preferred_element_type=jnp.float32)
        else:
            pb_ref[s] = jnp.broadcast_to(mass[s : s + 1, :], (size, size)).T


def collect(acc_ref, sum_ref):
    def body(s, carry):
        sum_ref[pl.ds(s, 1), :] = jnp.sum(acc_ref[s].T, axis=0, keepdims=True)
        return carry

    lax.fori_loop(0, acc_ref.shape[0], body, 0, unroll=32)


def fetch(points):
    refs, sources, sems = points
    if sources is not None:
        copies = [pltpu.make_async_copy(source, ref, sems.at[k]) for k, (source, ref) in enumerate(zip(sources, refs))]
        for copy in copies:
            copy.start()
        for copy in copies:
            copy.wait()
    return refs


def score(scores, lists, p):
    x_ref, y_ref, norm_ref = scores
    s, t = lists[p], lists[lists.shape[0] // 2 + p]
    cross = jnp.dot(x_ref[s], y_ref[t], preferred_element_type=jnp.float32)
    return s, t, cross * SCALE + norm_ref[pl.ds(t, 1), :]


def row_result(total, shift, valid, points, q_ref, lists, pairs, out_ref):
    blocks, size = out_ref.shape
    out_ref[...] = jnp.where(valid, jnp.log2(jnp.maximum(total, SMALL)) + shift, FLOOR)
    lowest = jnp.min(jnp.where(valid, total, 1.0))

    @pl.when(lowest < SMALL)
    def _():
        scores = fetch(points)

        def term(p):
            _, t, z = score(scores, lists, p)
            return z if q_ref is None else z + q_ref[pl.ds(t, 1), :]

        def block(s, first):
            def same(p):
                return (p < pairs) & (lists[jnp.minimum(p, pairs - 1)] == s)

            def raise_top(carry):
                return carry[0] + 1, jnp.maximum(carry[1], term(carry[0]))

            start = (first, jnp.full((size, size), 16.0 * FLOOR, jnp.float32))
            end, top = lax.while_loop(lambda carry: same(carry[0]), raise_top, start)
            top = jnp.max(top, axis=1, keepdims=True)

            def add(p, acc):
                return acc + jnp.exp2(term(p) - top)

            acc = lax.fori_loop(first, end, add, jnp.zeros((size, size), jnp.float32))
            full = top + jnp.log2(jnp.sum(acc, axis=1, keepdims=True))
            out_ref[pl.ds(s, 1), :] = jnp.broadcast_to(full, (size, size)).T[:1, :]
            return end

        lax.fori_loop(0, blocks, block, 0)
        out_ref[...] = jnp.where(valid, out_ref[...], FLOOR)


def normalised(potential, valid):
    held = jnp.where(valid, potential, FLOOR)
    top = jnp.max(jnp.max(held, axis=0, keepdims=True), axis=1, keepdims=True)
    return top, jnp.exp2(held - top)


def col_pass(k_ref, mass_ref, top_p, points, p_ref, touched_ref, lists, pairs, acc_ref, top_ref, out_ref):
    targets, size = out_ref.shape
    room = lists.shape[0] // 2
    acc_ref[...] = jnp.zeros_like(acc_ref)

    def chunk(c, carry):
        for k in range(CHUNK):
            s, t = lists[c * CHUNK + k], lists[room + c * CHUNK + k]
            acc_ref[eight(t), :] += halved(folded(k_ref[c * CHUNK + k] * mass_ref[s]))
        return carry

    lax.fori_loop(0, (pairs + CHUNK - 1) // CHUNK, chunk, 0)
    total = sum(every_eighth(acc_ref, r, targets) for r in range(8))
    valid = touched_ref[:targets, :] > 0.0
    out_ref[...] = jnp.where(valid, jnp.log2(jnp.maximum(total, SMALL)) + top_p, FLOOR)
    lowest = jnp.min(jnp.where(valid, total, 1.0))

    @pl.when(lowest < SMALL)
    def _():
        acc_ref[...] = jnp.zeros_like(acc_ref)
        top_ref[...] = jnp.full_like(top_ref, 16.0 * FLOOR)
        scores = fetch(points)

        def term(p):
            s, t, z = score(scores, lists, p)
            return t, z + jnp.broadcast_to(p_ref[pl.ds(s, 1), :], (size, size)).T

        def raise_top(p, carry):
            t, z = term(p)
            top_ref[eight(t), :] = jnp.maximum(top_ref[eight(t), :], jnp.max(folded(z), axis=0))
            return carry

        lax.fori_loop(0, pairs, raise_top, 0)
        top = functools.reduce(jnp.maximum, [every_eighth(top_ref, r, targets) for r in range(8)])
        out_ref[...] = top

        def add(p, carry):
            t, z = term(p)
            acc_ref[eight(t), :] += jnp.sum(folded(jnp.exp2(z - out_ref[pl.ds(t, 1), :])), axis=0)
            return carry

        lax.fori_loop(0, pairs, add, 0)
        exact = sum(every_eighth(acc_ref, r, targets) for r in range(8))
        out_ref[...] = jnp.where(valid, top + jnp.log2(jnp.maximum(exact, 1.0)), FLOOR)


def three_terms(row):
    high = row.astype(jnp.bfloat16)
    rest = row - high.astype(jnp.float32)
    middle = rest.astype(jnp.bfloat16)
    low = (rest - middle.astype(jnp.float32)).astype(jnp.bfloat16)
    return [high.astype(jnp.float32), middle.astype(jnp.float32), low.astype(jnp.float32)]


def extra_rows(row):
    place = lax.broadcasted_iota(jnp.int32, (EXTRA, row.shape[1]), 0)
    result = jnp.zeros(place.shape, jnp.float32)
    for k, term in enumerate(three_terms(row)):
        result = jnp.where(place == k, term, result)
    return result


def first_kernel(
    ssz_any, tsz_any, pat_any, cnt_any, xt_any, yt_any,
    k_ref, touched_ref, lists_smem, out_ref, x_any, y_any, norm_any,
    ssz_ref, tsz_ref, pat_ref, cnt_ref, xt_ref, x_ref, y_ref, norm_ref, part_ref, live_ref, acc_ref, sum_ref,
    sems, sems_out,
):
    blocks, size = out_ref.shape
    dims = xt_ref.shape[1]
    targets = yt_any.shape[0]
    slots = pat_ref.shape[0]
    room = lists_smem.shape[0] // 2
    small = [
        pltpu.make_async_copy(source, target, sems.at[k])
        for k, (source, target) in enumerate(
            [(ssz_any, ssz_ref), (tsz_any, tsz_ref), (pat_any, pat_ref), (cnt_any, cnt_ref)]
        )
    ]
    copy_x = pltpu.make_async_copy(xt_any, xt_ref, sems.at[4])
    middle = targets // 2
    copies_y = [
        pltpu.make_async_copy(
            yt_any.at[pl.ds(first, middle)], y_ref.at[pl.ds(first, middle), pl.ds(0, dims), :], sems.at[5 + k]
        )
        for k, first in enumerate((0, middle))
    ]
    for copy in small:
        copy.start()
    copy_x.start()
    for copy in copies_y:
        copy.start()
    acc_ref[...] = jnp.zeros_like(acc_ref)
    touched_ref[...] = jnp.zeros_like(touched_ref)
    lanes = lax.broadcasted_iota(jnp.int32, (1, size), 1)
    ones = (lax.broadcasted_iota(jnp.int32, (EXTRA, size), 0) < 3).astype(jnp.bfloat16)

    def pad_rows(t, carry):
        y_ref[t, pl.ds(dims, EXTRA), :] = ones
        return carry

    lax.fori_loop(0, targets, pad_rows, 0, unroll=16)
    y_ref[targets] = jnp.zeros(y_ref.shape[1:], jnp.bfloat16)
    norm_ref[pl.ds(targets, 8), :] = jnp.full((8, size), FLOOR, jnp.float32)
    for copy in small:
        copy.wait()
    copy_x.wait()

    def source(s):
        xt = xt_ref[s].astype(jnp.float32)
        live = lanes < ssz_ref[s]
        norm = jnp.where(live, -0.5 * jnp.sum(xt * xt, axis=0, keepdims=True), FLOOR)
        live_ref[pl.ds(s, 1), :] = live.astype(jnp.float32)
        x_ref[s] = jnp.concatenate([xt, extra_rows(norm)], axis=0).T.astype(jnp.bfloat16)

    def target(t):
        yt = y_ref[t, pl.ds(0, dims), :].astype(jnp.float32)
        part_ref[eight(t), :] = jnp.sum(folded(yt * yt), axis=0)

    def list_block(s, p):
        count = cnt_ref[s]
        for k in range(slots):
            lists_smem[p] = s
            lists_smem[room + p] = pat_ref[k, s]
            p = p + (k < count).astype(jnp.int32)
        return p

    half = blocks // 2

    def with_sources(s, p):
        source(2 * s)
        source(2 * s + 1)
        return list_block(s, p)

    def with_targets(s, p):
        for k in range(targets // half):
            target(s * (targets // half) + k)
        return list_block(half + s, p)

    pairs = lax.fori_loop(0, half, with_sources, 0, unroll=16)
    for k, copy in enumerate(copies_y):
        copy.wait()
        pairs = lax.fori_loop(k * (half // 2), (k + 1) * (half // 2), with_targets, pairs, unroll=8)
    for k in range(CHUNK):
        lists_smem[pairs + k] = blocks - 1
        lists_smem[room + pairs + k] = targets
    lists_smem[room - 1] = pairs
    sizes = jnp.broadcast_to(tsz_ref[...].astype(jnp.float32), (size, targets)).T
    mask = lax.broadcasted_iota(jnp.int32, (targets, size), 1).astype(jnp.float32) < sizes
    norms = sum(every_eighth(part_ref, r, targets) for r in range(8))
    norm_ref[pl.ds(0, targets), :] = jnp.where(mask, (-0.5 * SCALE) * norms, FLOOR)

    copies_out = [
        pltpu.make_async_copy(source, target, sems_out.at[k])
        for k, (source, target) in enumerate([(x_ref, x_any), (y_ref, y_any), (norm_ref, norm_any)])
    ]
    for copy in copies_out:
        copy.start()

    def chunk(first, count):
        for k in range(count):
            s, t = lists_smem[first + k], lists_smem[room + first + k]
            z = jnp.dot(x_ref[s], y_ref[t], preferred_element_type=jnp.float32) * SCALE + norm_ref[pl.ds(t, 1), :]
            mass = jnp.exp2(z)
            k_ref[first + k] = mass
            acc_ref[s] += mass
            touched_ref[pl.ds(t, 1), :] = jnp.ones((1, size), jnp.float32)

    whole = pairs // LARGE_CHUNK

    def large(c, carry):
        chunk(c * LARGE_CHUNK, LARGE_CHUNK)
        return carry

    def rest(c, carry):
        chunk(whole * LARGE_CHUNK + c * CHUNK, CHUNK)
        return carry

    lax.fori_loop(0, whole, large, 0)
    lax.fori_loop(0, (pairs - whole * LARGE_CHUNK + CHUNK - 1) // CHUNK, rest, 0)
    touched_ref[pl.ds(0, targets), :] = jnp.where(mask, touched_ref[pl.ds(0, targets), :], 0.0)
    collect(acc_ref, sum_ref)
    valid = live_ref[...] > 0.0
    points = ((x_ref, y_ref, norm_ref), None, None)
    row_result(sum_ref[...], 0.0, valid, points, None, lists_smem, pairs, out_ref)
    for copy in copies_out:
        copy.wait()


def col_kernel(n_parts, last, lists_smem, k_ref, touched_ref, logw_ref, x_any, y_any, norm_any, *rest):
    parts, rest = rest[:n_parts], rest[n_parts:]
    if last:
        field_any, out_ref, field_ref, *rest = rest
    else:
        out_ref, *rest = rest
    p_ref, mass_ref, acc_ref, top_ref, x_ref, y_ref, norm_ref, sems = rest
    valid, total = merged([part[...] for part in parts])
    p = jnp.where(valid, LOG2E * logw_ref[...] - total, 0.0)
    if last:
        field_ref[...] = p * FIELD
        copy_field = pltpu.make_async_copy(field_ref, field_any, sems.at[1])
        copy_field.start()
    top_p, mass = normalised(p, valid)
    spread(mass, mass_ref)
    p_ref[...] = p
    room = lists_smem.shape[0] // 2
    points = ((x_ref, y_ref, norm_ref), (x_any, y_any, norm_any), sems)
    col_pass(
        k_ref, mass_ref, top_p, points, p_ref, touched_ref, lists_smem, lists_smem[room - 1],
        acc_ref, top_ref, out_ref,
    )
    if last:
        copy_field.wait()


def row_kernel(n_parts, lists_smem, k_ref, earlier_ref, logw_ref, x_any, y_any, norm_any, *rest):
    parts, rest = rest[:n_parts], rest[n_parts:]
    out_ref, q_ref, mass_ref, acc_ref, sum_ref, x_ref, y_ref, norm_ref, sems = rest
    targets, size = logw_ref.shape
    valid, total = merged([part[...] for part in parts])
    q = jnp.where(valid, LOG2E * logw_ref[...] - total, 0.0)
    q_ref[...] = q
    top_q, mass = normalised(q, valid)
    mass_ref[pl.ds(0, targets), :] = mass
    mass_ref[pl.ds(targets, 8), :] = jnp.zeros((8, size), jnp.float32)
    acc_ref[...] = jnp.zeros_like(acc_ref)
    room = lists_smem.shape[0] // 2
    pairs = lists_smem[room - 1]

    def chunk(c, carry):
        for k in range(CHUNK):
            s, t = lists_smem[c * CHUNK + k], lists_smem[room + c * CHUNK + k]
            acc_ref[s] += k_ref[c * CHUNK + k] * mass_ref[pl.ds(t, 1), :]
        return carry

    lax.fori_loop(0, (pairs + CHUNK - 1) // CHUNK, chunk, 0)
    collect(acc_ref, sum_ref)
    points = ((x_ref, y_ref, norm_ref), (x_any, y_any, norm_any), sems)
    row_result(sum_ref[...], top_q, earlier_ref[...] > ABSENT, points, q_ref, lists_smem, pairs, out_ref)


def last_kernel(n_parts, logw_ref, *rest):
    parts, (out_ref,) = rest[:n_parts], rest[n_parts:]
    valid, total = merged([part[...] for part in parts])
    out_ref[...] = jnp.where(valid, (LOG2E * logw_ref[...] - total) * FIELD, 0.0)


def call(kernel, name, outs, scratch, args, spaces="v", spaces_out="v"):
    where = {"v": pltpu.VMEM, "h": pltpu.HBM, "s": pltpu.SMEM}
    return pl.pallas_call(
        kernel,
        out_shape=outs,
        in_specs=[pl.BlockSpec(memory_space=where[k]) for k in (spaces * len(args))[: len(args)]],
        out_specs=[pl.BlockSpec(memory_space=where[k]) for k in (spaces_out * len(outs))[: len(outs)]],
        scratch_shapes=scratch,
        name=name,
        compiler_params=pltpu.CompilerParams(vmem_limit_bytes=VMEM_LIMIT),
    )(*args)


def in_hbm(array):
    return pltpu.with_memory_space_constraint(array, pltpu.HBM)


def exchanged(part, axis):
    size = lax.axis_size(axis)
    pieces = [part]
    for d in range(1, size):
        if size & (size - 1):
            pairs = [(i, (i + d) % size) for i in range(size)]
        else:
            pairs = [(i, i ^ d) for i in range(size)]
        pieces.append(lax.ppermute(part, axis, pairs))
    return pieces


def on_device(src_points, tgt_points, src_logw, tgt_logw, src_sizes, tgt_sizes, pattern, counts):
    blocks, size, dims = src_points.shape
    targets = tgt_points.shape[0]
    slots = pattern.shape[2]
    f32, i32, bf16 = jnp.float32, jnp.int32, jnp.bfloat16
    xt = jnp.swapaxes(src_points, 1, 2)
    yt = jnp.swapaxes(tgt_points, 1, 2)
    room = -(-(blocks * slots + CHUNK + 1) // 512) * 512
    struct = jax.ShapeDtypeStruct
    dma = pltpu.SemaphoreType.DMA
    wide = pltpu.VMEM((blocks, size, size), f32)
    sums = pltpu.VMEM((blocks, size), f32)
    acc_col = pltpu.VMEM(((targets + 8) * 8, size), f32)
    lists_smem = pltpu.SMEM((2 * room,), i32)

    points_vmem = [
        pltpu.VMEM((blocks, size, dims + EXTRA), bf16),
        pltpu.VMEM((targets + 1, dims + EXTRA, size), bf16),
        pltpu.VMEM((targets + 8, size), f32),
    ]

    k, touched, lists, row_part, *points = call(
        first_kernel,
        "kernel_and_rows",
        [
            struct((blocks * slots + CHUNK, size, size), f32),
            struct((targets + 8, size), f32),
            pltpu.SMEM((2 * room,), i32),
            struct((blocks, size), f32),
            pltpu.HBM((blocks, size, dims + EXTRA), bf16),
            pltpu.HBM((targets + 1, dims + EXTRA, size), bf16),
            pltpu.HBM((targets + 8, size), f32),
        ],
        [
            pltpu.SMEM((blocks,), i32),
            pltpu.VMEM((1, targets), i32),
            pltpu.SMEM((slots, blocks), i32),
            pltpu.SMEM((blocks,), i32),
            pltpu.VMEM((blocks, dims, size), bf16),
            *points_vmem,
            pltpu.VMEM((targets * 8, size), f32),
            sums,
            wide,
            sums,
            dma((7,)),
            dma((3,)),
        ],
        [
            in_hbm(array)
            for array in (src_sizes, tgt_sizes[None, :], pattern[:, 0, :].T, counts[:, 0], xt, yt)
        ],
        "h",
        "vvsvhhh",
    )
    first_part = row_part
    points = [in_hbm(array) for array in points]
    for repeat in range(ITERS):
        last = repeat == ITERS - 1
        row_parts = exchanged(row_part, "col")
        *field_f, col_part = call(
            functools.partial(col_kernel, len(row_parts), last),
            "columns",
            ([struct((blocks, size), f32)] if last else []) + [struct((targets, size), f32)],
            ([sums] if last else []) + [sums, wide, acc_col, acc_col, *points_vmem, dma((3,))],
            [lists, k, touched, src_logw, *points, *row_parts],
            "svvvhhh" + "v" * len(row_parts),
            spaces_out="hv" if last else "v",
        )
        col_parts = exchanged(col_part, "row")
        if not last:
            (row_part,) = call(
                functools.partial(row_kernel, len(col_parts)),
                "rows",
                [struct((blocks, size), f32)],
                [
                    pltpu.VMEM((targets, size), f32),
                    pltpu.VMEM((targets + 8, size), f32),
                    wide,
                    sums,
                    *points_vmem,
                    dma((3,)),
                ],
                [lists, k, first_part, tgt_logw, *points, *col_parts],
                "svvvhhh" + "v" * len(col_parts),
            )
    (field_g,) = call(
        functools.partial(last_kernel, len(col_parts)),
        "target_field",
        [struct((targets, size), f32)],
        [],
        [tgt_logw] + col_parts,
    )
    return field_f[0], field_g


def solution(mesh):
    return jax.shard_map(
        on_device,
        mesh=mesh,
        in_specs=(
            P(("groups", "row"), None, None),
            P(("groups", "col"), None, None),
            P(("groups", "row"), None),
            P(("groups", "col"), None),
            P(("groups", "row")),
            P(("groups", "col")),
            P(("groups", "row"), "col", None),
            P(("groups", "row"), "col"),
        ),
        out_specs=(P(("groups", "row"), None), P(("groups", "col"), None)),
        check_vma=False,
    )
```
